32 devices in a mesh: half: 2 (over x), dp: 16 (over z, y, core).
Axes of the slice: x: 2, y: 2, z: 4, core: 2. Of those that a mesh axis runs over, the one named last changes fastest.
Arguments:
- tokens: bfloat16 [2, 16, 1024, 512], P('half', 'dp'), may hold values from -6 to 6
- cotangent: float32 [2, 16, 1024, 512], P('half', 'dp'), may hold values from -6 to 6
- lengths: int32 [2, 16, 16], P(None, 'dp'), may hold values from 1 to 256, 1024 in all within a row
- halting: int32 [2, 16, 1024], P('half', 'dp'), may hold values 0 or 1
- attention_in: bfloat16 [2, 512, 1536], P('half'), may hold values from -0.25 to 0.25
- attention_out: bfloat16 [2, 512, 512], P('half'), may hold values from -1 to 1
- cross_first: bfloat16 [2, 512, 512], P('half'), may hold values from -0.25 to 0.25
- cross_second: bfloat16 [2, 512, 512], P('half'), may hold values from -0.5 to 0.5
- expand_weight: bfloat16 [2, 512, 2048], P('half'), may hold values from -0.25 to 0.25
- expand_bias: float32 [2, 2048], P('half'), may hold values from -3 to 3
- contract_weight: bfloat16 [2, 2048, 512], P('half'), may hold values from -0.125 to 0.125
- contract_bias: float32 [2, 512], P('half'), may hold values from -2 to 2
- norm_gain: float32 [2, 3, 512], P('half'), may hold values from 0.25 to 1.75
- norm_bias: float32 [2, 3, 512], P('half'), may hold values from -1.2 to 1.2
Outputs:
- outputs: float32 [2, 16, 1024, 512], P('half', 'dp')
- input_grad: float32 [2, 16, 1024, 512], P('half', 'dp')
- attention_in_grad: float32 [2, 512, 1536], P('half')
- attention_out_grad: float32 [2, 512, 512], P('half')
- cross_first_grad: float32 [2, 512, 512], P('half')
- cross_second_grad: float32 [2, 512, 512], P('half')
- expand_weight_grad: float32 [2, 512, 2048], P('half')
- expand_bias_grad: float32 [2, 2048], P('half')
- contract_weight_grad: float32 [2, 2048, 512], P('half')
- contract_bias_grad: float32 [2, 512], P('half')
- norm_gain_grad: float32 [2, 3, 512], P('half')
- norm_bias_grad: float32 [2, 3, 512], P('half')
The draws below stay inside these ranges and needn't reach their ends.
All inputs are finite; a program needn't handle non-finite values. No bound on the sum of `halting` on one device may be relied on, other than what follows from the above.
Results may differ from the reference program's by a relative error of at most 0.024.
Values may be sent and summed in bfloat16 or wider, within the bound.
No kernel may reach another device: no remote copies, remote signals or barrier semaphores. Data moves between devices by JAX's collectives and lax.ppermute only.
A program may use at most 192 MiB of HBM per device.

```python
import math
import jax
import jax.numpy as jnp
import numpy as np
from jax import lax

D = 512
HEADS = 8
FF = 2048
LEN = 1024
SEGS = 16
STEP = 2
MOST = 256
ROWS = 16


def touch_ends(values, key, least, top_value):
    shape = values.shape
    index_at = [jax.random.randint(jax.random.fold_in(key, axis), (), 0, shape[axis]) for axis in range(len(shape))]
    values = values.at[tuple(index_at)].set(least)
    longest = shape.index(max(shape))
    index_at[longest] = (index_at[longest] + 1) % shape[longest]
    return values.at[tuple(index_at)].set(top_value)


def block_levels(own_key, shape, split, smallest, high):
    gain = 1.0
    for position, shards_of in split:
        draws = jax.random.uniform(jax.random.fold_in(jax.random.fold_in(own_key, 6), position), (shards_of,), jnp.float32, smallest / len(split), high / len(split))
        gain = gain * jnp.repeat(jnp.exp(draws), shape[position] // shards_of).reshape((-1,) + (1,) * (len(shape) - 1 - position))
    return gain


def split_up(amount, total, most, slope):
    loads = [(1 << 20) // math.isqrt(rank ** slope) + 1 for rank in range(2, amount + 1)]
    rest, holding = total - most - (amount - 1), [1] * (amount - 1)
    while rest > 0:
        free = [i for i in range(amount - 1) if holding[i] < most]
        mass, left = sum([loads[i] for i in free]), rest
        for i in free:
            extra = min(most - holding[i], max(1, left * loads[i] // mass), rest)
            holding[i] = holding[i] + extra
            rest = rest - extra
    return np.array([most] + holding)


def uneven_parts(rng, amount, total, most, skew):
    if amount == 2:
        one = jax.random.randint(rng, (), max(1, total - most), min(most, total - 1) + 1)
        return jnp.stack([one, total - one])
    tallies = jnp.asarray(split_up(amount, total, most, skew), jnp.int32)
    pairs = (amount - 1) // 2
    giver, receiver = tallies[1:1 + 2 * pairs:2], tallies[2:2 + 2 * pairs:2]
    slack = jnp.minimum(giver - 1, most - receiver)
    moved = jax.random.randint(jax.random.fold_in(rng, 1), (pairs,), 0, 1 << 20) % (slack + 1)
    tallies = tallies.at[1:1 + 2 * pairs:2].set(giver - moved).at[2:2 + 2 * pairs:2].set(receiver + moved)
    return tallies[jax.random.permutation(jax.random.fold_in(rng, 2), amount)]


def normal_values(own_key, extent, scale, most, pieces=(), kind=jnp.bfloat16):
    entries = jax.random.normal(own_key, extent, jnp.float32) * scale
    if len(pieces) > 0:
        entries = block_levels(own_key, extent, pieces, -0.22, 0.18) * entries
    return jnp.clip(entries, min=-most, max=most).astype(kind)


def setup_inputs(seed: int = 0) -> dict:
    splits = jax.random.split(jax.random.key(seed), 15)
    return {
        "tokens": normal_values(splits[0], (2, ROWS, LEN, D), 1.0, 6.0, ((0, 2), (1, 16))),
        "cotangent": normal_values(splits[1], (2, ROWS, LEN, D), 1.0, 6.0, ((0, 2), (1, 16)), jnp.float32),
        "lengths": jax.vmap(lambda own: uneven_parts(own, SEGS, LEN, MOST, 2))(jax.random.split(splits[2], 2 * ROWS)).reshape((2, ROWS, SEGS)).astype(jnp.int32),
        "halting": touch_ends((jax.random.randint(splits[3], (2, ROWS, LEN), 0, 4) < 3).astype(jnp.int32), jax.random.fold_in(splits[3], 1), 0, 1),
        "attention_in": normal_values(splits[4], (2, D, 3 * D), D ** -0.5, 0.25, ((0, 2),)),
        "attention_out": normal_values(splits[5], (2, D, D), (D // 16) ** -0.5, 1.0, ((0, 2),)),
        "cross_first": normal_values(splits[6], (2, D, D), D ** -0.5, 0.25, ((0, 2),)),
        "cross_second": normal_values(splits[7], (2, D, D), (D // 4) ** -0.5, 0.5, ((0, 2),)),
        "expand_weight": normal_values(splits[8], (2, D, FF), D ** -0.5, 0.25, ((0, 2),)),
        "expand_bias": normal_values(splits[9], (2, FF), 0.5, 3.0, ((0, 2),), jnp.float32),
        "contract_weight": normal_values(splits[10], (2, FF, D), FF ** -0.5, 0.125, ((0, 2),)),
        "contract_bias": normal_values(splits[11], (2, D), 0.3, 2.0, ((0, 2),), jnp.float32),
        "norm_gain": jnp.clip(1.0 + 0.15 * jax.random.normal(splits[12], (2, 3, D), jnp.float32), 0.25, 1.75),
        "norm_bias": normal_values(splits[13], (2, 3, D), 0.2, 1.2, ((0, 2),), jnp.float32),
    }


@jax.custom_vjp
def low(v):
    return lax.optimization_barrier(v.astype(jnp.bfloat16)).astype(jnp.float32)

@jax.custom_vjp
def low_back(v):
    return v

def low_keep(v):
    return (low(v), None)

def low_pass(kept, grad):
    return (grad,)

def back_keep(v):
    return (v, None)

def back_low(kept, grad):
    return (low(grad),)
low.defvjp(low_keep, low_pass)
low_back.defvjp(back_keep, back_low)
EPSILON = 1e-06

def product(left, right):
    return jnp.dot(left, right, preferred_element_type=jnp.float32, precision=lax.Precision.HIGHEST)

def layer_norm(summed, gain_row, shift_row):
    center = summed - lax.optimization_barrier(jnp.mean(summed, axis=-1, keepdims=True))
    spread = lax.optimization_barrier(jnp.mean(center * center, axis=-1, keepdims=True))
    return center * lax.rsqrt(spread + EPSILON) * gain_row + shift_row

def positions(lengths_row, length):
    endings = jnp.cumsum(lengths_row).astype(jnp.int32)
    places = jnp.arange(length, dtype=jnp.int32)
    passed = (places[:, None] >= endings[None, :]).astype(jnp.int32)
    segment = lax.optimization_barrier(jnp.sum(passed, axis=1)).astype(jnp.int32)
    begins = lax.optimization_barrier(jnp.sum(passed * lengths_row[None, :], axis=1)).astype(jnp.int32)
    return (segment, places - begins)

def timing(places, model_width):
    half_width = model_width // 2
    frequency = jnp.exp(jnp.arange(half_width, dtype=jnp.float32) * (-math.log(10000.0) / half_width))
    angles = places[..., None] * frequency
    return jnp.concatenate([jnp.sin(angles), jnp.cos(angles)], axis=-1)

def attend(queries, keys, values, allowed):
    length, model_width = queries.shape
    key_count = keys.shape[0]
    head_size = model_width // HEADS
    query_heads = queries.reshape(length, HEADS, head_size)
    key_heads = keys.reshape(key_count, HEADS, head_size)
    value_heads = values.reshape(key_count, HEADS, head_size)
    scores = jnp.einsum('qhd,khd->hqk', query_heads, key_heads, precision=lax.Precision.HIGHEST) * (1.0 / math.sqrt(head_size))
    scores = low_back(jnp.where(allowed[None], scores, -jnp.inf))
    probs_low = low(jax.nn.softmax(scores, axis=-1))
    mixed_out = jnp.einsum('hqk,khd->qhd', probs_low, value_heads, precision=lax.Precision.HIGHEST)
    return mixed_out.reshape(length, model_width)

def self_block(start, weight_in, weight_out, gain_row, shift_row, allowed):
    model_width = start.shape[-1]
    projected = low(low_back(product(low(start), weight_in)))
    attended = attend(projected[:, :model_width], projected[:, model_width:2 * model_width], projected[:, 2 * model_width:], allowed)
    branch = low_back(product(low(low_back(attended)), weight_out))
    return layer_norm(start + branch, gain_row, shift_row)

def ffn_block(inputs, expand_w, expand_b, contract_w, contract_b, gain_row, shift_row):
    before = low_back(product(low(inputs), expand_w) + expand_b)
    hidden = low(jax.nn.gelu(before, approximate=True))
    branch = low_back(product(hidden, contract_w) + contract_b)
    return layer_norm(inputs + branch, gain_row, shift_row)

def pair_forward(source, target, source_lengths, target_lengths, source_halt, target_halt, weights):
    weight_in, weight_out, cross_one, cross_two, expand_w, expand_b, contract_w, contract_b, gain_all, shift_all = weights
    model_width = source.shape[-1]
    source_segment, source_place = positions(source_lengths, LEN)
    target_segment, target_place = positions(target_lengths, LEN)
    step_signal = timing(jnp.asarray(STEP, jnp.float32), model_width)
    places = jnp.arange(LEN, dtype=jnp.int32)
    source_allowed = source_segment[:, None] == source_segment[None, :]
    target_allowed = (target_segment[:, None] == target_segment[None, :]) & (places[:, None] >= places[None, :])
    cross_allowed = target_segment[:, None] == source_segment[None, :]
    source_start = source + timing(source_place.astype(jnp.float32), model_width) + step_signal
    source_first = self_block(source_start, weight_in[0], weight_out[0], gain_all[0, 0], shift_all[0, 0], source_allowed)
    source_ffn = ffn_block(source_first, expand_w[0], expand_b[0], contract_w[0], contract_b[0], gain_all[0, 1], shift_all[0, 1])
    source_halt_f = source_halt.astype(jnp.float32)[:, None]
    stepped = source + source_halt_f * (source_ffn - source)
    memory = layer_norm(stepped, gain_all[0, 2], shift_all[0, 2])
    memory_low = low(memory)
    keys = low(low_back(product(memory_low, cross_one[0])))
    values = low(low_back(product(memory_low, cross_two[0])))
    target_start = target + timing(target_place.astype(jnp.float32), model_width) + step_signal
    target_first = self_block(target_start, weight_in[1], weight_out[1], gain_all[1, 0], shift_all[1, 0], target_allowed)
    queries = low(low_back(product(low(target_first), cross_one[1])))
    crossed = attend(queries, keys, values, cross_allowed)
    cross_branch = low_back(product(low(low_back(crossed)), cross_two[1]))
    second = layer_norm(target_first + cross_branch, gain_all[1, 2], shift_all[1, 2])
    target_ffn = ffn_block(second, expand_w[1], expand_b[1], contract_w[1], contract_b[1], gain_all[1, 1], shift_all[1, 1])
    target_halt_f = target_halt.astype(jnp.float32)[:, None]
    result = target + target_halt_f * (target_ffn - target)
    return (memory, result)

def reference(tokens, cotangent, lengths, halting, attention_in, attention_out, cross_first, cross_second, expand_weight, expand_bias, contract_weight, contract_bias, norm_gain, norm_bias):
    weights = tuple((array.astype(jnp.float32) for array in (attention_in, attention_out, cross_first, cross_second, expand_weight, expand_bias, contract_weight, contract_bias, norm_gain, norm_bias)))
    states = tokens.astype(jnp.float32)
    grads_in = cotangent.astype(jnp.float32)

    def row_step(totals, packed):
        source, target, grad_source, grad_target, source_lengths, target_lengths, source_halt, target_halt = packed

        def forward(source_in, target_in, weight_set):
            return pair_forward(source_in, target_in, source_lengths, target_lengths, source_halt, target_halt, weight_set)
        results, backward = jax.vjp(forward, source, target, weights)
        back_source, back_target, back_weights = backward((grad_source, grad_target))
        totals = jax.tree.map(jnp.add, totals, back_weights)
        return (totals, (results[0], results[1], back_source, back_target))
    zeros = jax.tree.map(jnp.zeros_like, weights)
    packed = (states[0], states[1], grads_in[0], grads_in[1], lengths[0], lengths[1], halting[0], halting[1])
    totals, (memory, result, back_source, back_target) = lax.scan(row_step, zeros, packed)
    outputs = jnp.stack([memory, result])
    input_grad = jnp.stack([back_source, back_target])
    return (outputs, input_grad, totals[0], totals[1], totals[2], totals[3], totals[4], totals[5], totals[6], totals[7], totals[8], totals[9])
```

```python
from functools import partial
import math

import jax
import jax.numpy as jnp
from jax import lax
from jax.experimental import pallas as pl
from jax.experimental.pallas import tpu as pltpu
from jax.sharding import PartitionSpec as P

HEADS = 8
STEP = 2
EPSILON = 1e-06
LONGEST = 256
ROWS = 256
KEYS = 128
PIECE = 512
MASKED = -1e30
VMEM_BYTES = 60 * 1024 * 1024
F32 = jnp.float32
BF16 = jnp.bfloat16


def mul(left, right):
    return jnp.dot(left, right, preferred_element_type=F32)


def mul_nt(left, right):
    return lax.dot_general(left, right, (((1,), (1,)), ((), ())), preferred_element_type=F32)


def iota(shape, axis):
    return lax.broadcasted_iota(jnp.int32, shape, axis)


def norm_parts(summed):
    center = summed - jnp.mean(summed, axis=-1, keepdims=True)
    rate = lax.rsqrt(jnp.mean(center * center, axis=-1, keepdims=True) + EPSILON)
    return center * rate, rate


def norm_back(grad, unit, rate, gain):
    scaled = grad * gain
    return rate * (
        scaled
        - jnp.mean(scaled, axis=-1, keepdims=True)
        - unit * jnp.mean(scaled * unit, axis=-1, keepdims=True)
    )


def gate(before):
    inner = math.sqrt(2.0 / math.pi) * (before + 0.044715 * before * before * before)
    half_one = 0.5 * (1.0 + jnp.tanh(inner))
    return before * half_one


def gate_and_slope(before):
    scale = math.sqrt(2.0 / math.pi)
    square = before * before
    bent = jnp.tanh(scale * before * (1.0 + 0.044715 * square))
    half_one = 0.5 + 0.5 * bent
    slope = half_one + 0.5 * before * (1.0 - bent * bent) * (
        scale * (1.0 + 3 * 0.044715 * square)
    )
    return before * half_one, slope


def bounds(lengths, side, key_side, block, causal):
    first_row = block * ROWS
    last_row = first_row + ROWS - 1
    place = first_row + iota((1, ROWS), 1)
    low = jnp.zeros((1, ROWS), jnp.int32)
    high = jnp.zeros((1, ROWS), jnp.int32)
    least = jnp.int32(0)
    most = jnp.int32(0)
    at = jnp.int32(0)
    key_at = jnp.int32(0)
    for k in range(lengths.shape[1]):
        end = at + lengths[side, k]
        key_end = key_at + lengths[key_side, k]
        inside = (place >= at) & (place < end)
        low = jnp.where(inside, key_at, low)
        high = jnp.where(inside, key_end, high)
        least = jnp.where((first_row >= at) & (first_row < end), key_at, least)
        most = jnp.where((last_row >= at) & (last_row < end), key_end, most)
        at, key_at = end, key_end
    if causal is not None:
        high = jnp.where(causal, jnp.minimum(high, place + 1), high)
        most = jnp.where(causal, jnp.minimum(most, last_row + 1), most)
    return low, high, least // KEYS, (most + KEYS - 1) // KEYS


def keep_pair(block, axis):
    place = iota(block.shape, axis)
    half = block.shape[axis] // 2
    zero = jnp.zeros_like(block)
    return jnp.concatenate(
        [jnp.where(place < half, block, zero), jnp.where(place >= half, block, zero)],
        axis=1 - axis,
    )


def split_heads(source, stacked, pairs):
    block, base = source
    for p in range(pairs):
        for t in range(ROWS // KEYS):
            part = block[t * KEYS : (t + 1) * KEYS, p * 128 : (p + 1) * 128]
            stacked[p, base + t] = keep_pair(part, 1)


def split_heads_turned(source, stacked, pairs):
    block, base = source
    turned = block.T
    for p in range(pairs):
        for t in range(ROWS // KEYS):
            part = turned[p * 128 : (p + 1) * 128, t * KEYS : (t + 1) * KEYS]
            stacked[p, base + t] = keep_pair(part, 0)


def mask_bias(block_index, low, high):
    key_place = block_index * KEYS + iota((KEYS, ROWS), 0)
    return jnp.where((key_place >= low) & (key_place < high), 0.0, MASKED)


def attend_block(queries, keys, values_turned, span, mixed, top, total):
    low, high, least, most = span
    pairs = keys.shape[0]
    mixed[...] = jnp.zeros_like(mixed)
    top[...] = jnp.full(top.shape, MASKED, F32)
    total[...] = jnp.zeros_like(total)

    def one(j, carried):
        bias = mask_bias(j, low, high)
        for p in range(pairs):
            scores = mul_nt(keys[p, j], queries[:, p * 128 : (p + 1) * 128])
            weights, fades = [], []
            for u in range(2):
                h = 2 * p + u
                part = scores[u * KEYS : (u + 1) * KEYS] + bias
                old = top[h : h + 1, :]
                new = jnp.maximum(old, jnp.max(part, axis=0, keepdims=True))
                fade = jnp.exp(old - new)
                weight = jnp.exp(part - new)
                total[h : h + 1, :] = total[h : h + 1, :] * fade + jnp.sum(
                    weight, axis=0, keepdims=True
                )
                top[h : h + 1, :] = new
                weights.append(weight.astype(BF16))
                fades.append(fade)
            added = mul(values_turned[p, j], jnp.concatenate(weights, axis=0))
            for u in range(2):
                at = p * 128 + u * 64
                mixed[at : at + 64, :] = (
                    mixed[at : at + 64, :] * fades[u] + added[u * 64 : (u + 1) * 64]
                )
        return carried

    lax.fori_loop(least, most, one, 0)
    for h in range(2 * pairs):
        rate = 1.0 / total[h : h + 1, :]
        mixed[h * 64 : (h + 1) * 64, :] = mixed[h * 64 : (h + 1) * 64, :] * rate
    top[...] = top[...] + jnp.log(total[...])


def attend_block_back(
    queries, grads, keys, keys_turned, values, span, logs, inner, grad_queries, grad_keys, grad_values
):
    low, high, least, most = span
    pairs = keys.shape[0]
    grad_queries[...] = jnp.zeros_like(grad_queries)
    first_half = iota((KEYS, 128), 1) < 64

    def one(j, carried):
        bias = mask_bias(j, low, high)
        rows = pl.ds(pl.multiple_of(j * KEYS, KEYS), KEYS)
        for p in range(pairs):
            lanes = slice(p * 128, (p + 1) * 128)
            query = queries[:, lanes]
            grad = grads[:, lanes]
            scores = mul_nt(keys[p, j], query)
            grad_prob = mul_nt(values[p, j], grad)
            probs, grad_scores = [], []
            for u in range(2):
                h = 2 * p + u
                part = slice(u * KEYS, (u + 1) * KEYS)
                prob = jnp.exp(scores[part] + bias - logs[h : h + 1, :])
                probs.append(prob.astype(BF16))
                grad_scores.append((prob * (grad_prob[part] - inner[h : h + 1, :])).astype(BF16))
            prob_pair = jnp.concatenate(probs, axis=0)
            grad_pair = jnp.concatenate(grad_scores, axis=0)
            both = mul(prob_pair, grad)
            grad_values[rows, lanes] += jnp.where(first_half, both[:KEYS], both[KEYS:])
            both = mul(grad_pair, query)
            grad_keys[rows, lanes] += jnp.where(first_half, both[:KEYS], both[KEYS:])
            grad_queries[lanes, :] += mul(keys_turned[p, j], grad_pair)
        return carried

    lax.fori_loop(least, most, one, 0)


def row_inner(grads, mixed):
    width = grads.shape[1]
    head_of = iota((16, width), 1) // (width // HEADS)
    picks = (head_of == iota((16, width), 0)).astype(BF16)
    product = grads.astype(F32) * mixed.astype(F32)
    big = product.astype(BF16)
    small = (product - big.astype(F32)).astype(BF16)
    return mul_nt(picks, big) + mul_nt(picks, small)


def column(row):
    return jnp.broadcast_to(row, (128, row.shape[1])).T[:, :1]


class Copies:
    def __init__(self, sems):
        self.sems = sems
        self.used = 0

    def start(self, source, target):
        copy = pltpu.make_async_copy(source, target, self.sems.at[self.used])
        self.used += 1
        copy.start()
        return copy


def block_rows(i):
    return pl.ds(pl.multiple_of(i * ROWS, ROWS), ROWS)


def colsum(values):
    return jnp.sum(values, axis=0, keepdims=True)


def ffn_forward(low_in, base, weights):
    expand_w, expand_b, contract_w, contract_b = weights
    total = base + contract_b[...]
    for c in range(expand_w.shape[1] // PIECE):
        part = slice(c * PIECE, (c + 1) * PIECE)
        before = mul(low_in, expand_w[:, part]) + expand_b[:, part]
        total = total + mul(gate(before).astype(BF16), contract_w[part, :])
    return total


def ffn_forward_kept(low_in, base, weights, hidden, slopes):
    expand_w, expand_b, contract_w, contract_b = weights
    total = base + contract_b[...]
    for c in range(expand_w.shape[1] // PIECE):
        part = slice(c * PIECE, (c + 1) * PIECE)
        before = mul(low_in, expand_w[:, part]) + expand_b[:, part]
        gated, slope = gate_and_slope(before)
        gated = gated.astype(BF16)
        hidden(part, gated)
        slopes[:, part] = slope
        total = total + mul(gated, contract_w[part, :])
    return total


def ffn_back(grad_summed, weights, slopes, grad_before, small):
    expand_w, _, contract_w, _ = weights
    branch = grad_summed.astype(BF16)
    grad_in = grad_summed
    for c in range(expand_w.shape[1] // PIECE):
        part = slice(c * PIECE, (c + 1) * PIECE)
        pushed = (mul_nt(branch, contract_w[part, :]) * slopes[:, part]).astype(BF16)
        grad_before(part, pushed)
        small[8 + c : 9 + c, :] += colsum(pushed.astype(F32))
        grad_in = grad_in + mul_nt(pushed, expand_w[:, part])
    return branch, grad_in


def first_kernel(
    side_ref, lengths, tokens, halting, weight_in, weight_out, expand_w, expand_b, contract_w,
    contract_b, cross_w, value_w, gains, shifts,
    start_low, projected, attended, logs, first_sum, memory, memory_low,
    tok, win, wout, w1, w2, table_big, table_small, start, proj, keys, values_turned, mixed, top, total,
    att, fsum, mem, meml, slow, sems,
):
    side = side_ref[0]
    blocks = tokens.shape[0] // ROWS
    width = tokens.shape[1]
    pairs = width // 128
    cp = Copies(sems)
    c_tok = cp.start(tokens, tok)
    c_in = cp.start(weight_in, win)
    c_out = cp.start(weight_out, wout)
    c_w1 = cp.start(expand_w, w1)
    c_w2 = cp.start(contract_w, w2)

    half = width // 2
    rate = jnp.exp(iota((16, half), 1).astype(F32) * (-math.log(10000.0) / half))
    fine = iota((16, half), 0).astype(F32) * rate
    coarse = fine * 16.0
    fine_s, fine_c, coarse_s, coarse_c = jnp.sin(fine), jnp.cos(fine), jnp.sin(coarse), jnp.cos(coarse)
    step_s, step_c = fine_s[STEP : STEP + 1], fine_c[STEP : STEP + 1]
    for a in range(LONGEST // 16):
        s, c = coarse_s[a : a + 1], coarse_c[a : a + 1]
        whole = jnp.concatenate(
            [s * fine_c + c * fine_s + step_s, c * fine_c - s * fine_s + step_c], axis=1
        )
        big = whole.astype(BF16)
        table_big[a * 16 : (a + 1) * 16, :] = big
        table_small[a * 16 : (a + 1) * 16, :] = (whole - big.astype(F32)).astype(BF16)

    lane = iota((1, 128), 1)
    begins = jnp.zeros((1, 128), jnp.int32)
    at = jnp.int32(0)
    for k in range(lengths.shape[1]):
        begins = jnp.where(lane == k, at, begins)
        at = at + lengths[side, k]
    c_tok.wait()
    c_in.wait()

    def prepare(i, carried):
        rows = block_rows(i)
        place = i * ROWS + iota((ROWS, 1), 0)
        began = jnp.max(jnp.where(place >= begins, begins, 0), axis=1, keepdims=True)
        picks = (iota((ROWS, LONGEST), 1) == place - began).astype(F32).astype(BF16)
        block = tok[rows, :].astype(F32) + (mul(picks, table_big[...]) + mul(picks, table_small[...]))
        start[rows, :] = block
        low = block.astype(BF16)
        slow[rows, :] = low
        sent = mul(low, win[...]).astype(BF16)
        proj[rows, :] = sent
        split_heads((sent[:, width : 2 * width], 2 * i), keys, pairs)
        split_heads_turned((sent[:, 2 * width :], 2 * i), values_turned, pairs)
        return carried

    lax.fori_loop(0, blocks, prepare, 0)
    c_slow = cp.start(slow, start_low)
    c_proj = cp.start(proj, projected)
    c_out.wait()
    c_w1.wait()
    c_w2.wait()
    weights = (w1, expand_b, w2, contract_b)

    def attend(i, carried):
        rows = block_rows(i)
        queries = proj[rows, :width] * BF16(1.0 / math.sqrt(width // HEADS))
        attend_block(
            queries, keys, values_turned, bounds(lengths, side, side, i, side == 1), mixed, top, total
        )
        logs[i] = top[...]
        low = mixed[...].astype(BF16).T
        att[rows, :] = low
        summed = start[rows, :] + mul(low, wout[...])
        fsum[rows, :] = summed

        @pl.when(side == 0)
        def _():
            first = norm_parts(summed)[0] * gains[0:1, :] + shifts[0:1, :]
            tail = norm_parts(ffn_forward(first.astype(BF16), first, weights))[0] * gains[1:2, :] + shifts[1:2, :]
            state = tok[rows, :].astype(F32)
            running = column(halting[:, block_rows(i)].astype(F32))
            stepped = state + running * (tail - state)
            kept = norm_parts(stepped)[0] * gains[2:3, :] + shifts[2:3, :]
            mem[rows, :] = kept
            meml[rows, :] = kept.astype(BF16)

        return carried

    lax.fori_loop(0, blocks, attend, 0)
    c_att = cp.start(att, attended)
    c_fsum = cp.start(fsum, first_sum)

    @pl.when(side == 0)
    def _():
        a = cp.start(mem, memory)
        b = cp.start(meml, memory_low)
        a.wait()
        b.wait()

    for c in (c_slow, c_proj, c_att, c_fsum):
        c.wait()


ANY = pl.BlockSpec(memory_space=pl.ANY)
SMEM = pl.BlockSpec(memory_space=pltpu.SMEM)
VMEM = pl.BlockSpec(memory_space=pltpu.VMEM)


def shape(s, d):
    return jax.ShapeDtypeStruct(s, d)


def call(kernel, ins, outs, scratch, flops, moved, aliases=None, name=None):
    return pl.pallas_call(
        kernel,
        in_specs=ins,
        out_specs=[o[1] for o in outs],
        out_shape=[o[0] for o in outs],
        scratch_shapes=scratch,
        input_output_aliases=aliases or {},
        compiler_params=pltpu.CompilerParams(vmem_limit_bytes=VMEM_BYTES),
        cost_estimate=pl.CostEstimate(flops=flops, bytes_accessed=moved, transcendentals=0),
        name=name,
    )


def run_first(side, lengths, tokens, halting, weight_in, weight_out, expand_w, expand_b, contract_w, contract_b, cross_w, value_w, gains, shifts):
    n, d = tokens.shape
    ff = expand_w.shape[1]
    pairs, nk = d // 128, n // KEYS
    V = pltpu.VMEM
    return call(
        first_kernel,
        [SMEM, SMEM, ANY, VMEM, ANY, ANY, ANY, VMEM, ANY, VMEM, ANY, ANY, VMEM, VMEM],
        [
            (shape((n, d), BF16), ANY),
            (shape((n, 3 * d), BF16), ANY),
            (shape((n, d), BF16), ANY),
            (shape((n // ROWS, HEADS, ROWS), F32), VMEM),
            (shape((n, d), F32), ANY),
            (shape((n, d), F32), ANY),
            (shape((n, d), BF16), ANY),
        ],
        [
            V((n, d), BF16), V((d, 3 * d), BF16), V((d, d), BF16), V((d, ff), BF16), V((ff, d), BF16),
            V((LONGEST, d), BF16), V((LONGEST, d), BF16), V((n, d), F32), V((n, 3 * d), BF16),
            V((pairs, nk, 2 * KEYS, 128), BF16), V((pairs, nk, 128, 2 * KEYS), BF16),
            V((d, ROWS), F32), V((HEADS, ROWS), F32), V((HEADS, ROWS), F32),
            V((n, d), BF16), V((n, d), F32), V((n, d), F32), V((n, d), BF16), V((n, d), BF16),
            pltpu.SemaphoreType.DMA((11,)),
        ],
        12_000_000_000, 20_000_000, name="first_part",
    )(side, lengths, tokens, halting, weight_in, weight_out, expand_w, expand_b, contract_w, contract_b, cross_w, value_w, gains, shifts)


SMALL_ROWS = 16


def middle_kernel(
    side_ref, lengths, tokens, halting, cotangent, first_sum, memory_in, key_w, value_w, cross_w, mix_w,
    expand_w, expand_b, contract_w, contract_b, gains, shifts, memory,
    result, hidden, branch, grad_before, ffn_in, grad_first, grad_memory,
    pairs_low, crossed, grad_cross, first_low, grad_query, small,
    mlow, kw, vw, cw, mw, w1, w2, tok, cot, fsum, keys, keys_t, values, values_t, slopes,
    mixed, top, total, gqt, gk, gv, res, hid, bra, gbef, fin, gfirst, gmem, plow, cro, gcro, flow, gqry, sems,
):
    side = side_ref[0]
    n, width = tok.shape
    blocks = n // ROWS
    pairs = width // 128
    scale = 1.0 / math.sqrt(width // HEADS)

    @pl.when(side == 1)
    def _():
        cp = Copies(sems)
        c_mlow = cp.start(memory_in, mlow)
        c_kw, c_vw = cp.start(key_w, kw), cp.start(value_w, vw)
        rest = [
            cp.start(a, b)
            for a, b in (
                (cross_w, cw), (mix_w, mw), (first_sum, fsum), (expand_w, w1), (contract_w, w2),
                (tokens, tok), (cotangent, cot),
            )
        ]
        small[...] = jnp.zeros_like(small)
        gk[...] = jnp.zeros_like(gk)
        gv[...] = jnp.zeros_like(gv)
        c_mlow.wait()
        c_kw.wait()
        c_vw.wait()

        def prepare(i, carried):
            low = mlow[block_rows(i), :]
            key = mul(low, kw[...]).astype(BF16)
            value = mul(low, vw[...]).astype(BF16)
            split_heads((key, 2 * i), keys, pairs)
            split_heads((value, 2 * i), values, pairs)
            split_heads_turned((key, 2 * i), keys_t, pairs)
            split_heads_turned((value, 2 * i), values_t, pairs)
            return carried

        lax.fori_loop(0, blocks, prepare, 0)
        for c in rest:
            c.wait()
        weights = (w1, expand_b, w2, contract_b)

        def one(i, carried):
            rows = block_rows(i)
            first = norm_parts(fsum[rows, :])[0] * gains[0:1, :] + shifts[0:1, :]
            low = first.astype(BF16)
            flow[rows, :] = low
            queries = mul(low, cw[...]).astype(BF16) * BF16(scale)
            span = bounds(lengths, 1, 0, i, None)
            attend_block(queries, keys, values_t, span, mixed, top, total)
            mix_low = mixed[...].astype(BF16).T
            cro[rows, :] = mix_low
            unit2, rate2 = norm_parts(first + mul(mix_low, mw[...]))
            second = unit2 * gains[2:3, :] + shifts[2:3, :]
            low = second.astype(BF16)
            fin[rows, :] = low

            def keep_hidden(part, value):
                hid[rows, part] = value

            def keep_before(part, value):
                gbef[rows, part] = value

            unit1, rate1 = norm_parts(ffn_forward_kept(low, second, weights, keep_hidden, slopes))
            state = tok[rows, :].astype(F32)
            running = column(halting[:, block_rows(i)].astype(F32))
            res[rows, :] = state + running * (unit1 * gains[1:2, :] + shifts[1:2, :] - state)
            grad = running * cot[rows, :]
            small[1:2, :] += colsum(grad * unit1)
            small[4:5, :] += colsum(grad)
            grad_low, grad = ffn_back(
                norm_back(grad, unit1, rate1, gains[1:2, :]), weights, slopes, keep_before, small
            )
            bra[rows, :] = grad_low
            small[6:7, :] += colsum(grad_low.astype(F32))
            small[2:3, :] += colsum(grad * unit2)
            small[5:6, :] += colsum(grad)
            grad = norm_back(grad, unit2, rate2, gains[2:3, :])
            grad_low = grad.astype(BF16)
            gcro[rows, :] = grad_low
            grad_mix = mul_nt(grad_low, mw[...]).astype(BF16)
            attend_block_back(
                queries, grad_mix, keys, keys_t, values, span, top, row_inner(grad_mix, mix_low), gqt, gk, gv
            )
            grad_low = (gqt[...] * scale).astype(BF16).T
            gqry[rows, :] = grad_low
            gfirst[rows, :] = grad + mul_nt(grad_low, cw[...])
            return carried

        lax.fori_loop(0, blocks, one, 0)

        def finish(i, carried):
            rows = block_rows(i)
            key = gk[rows, :].astype(BF16)
            value = gv[rows, :].astype(BF16)
            plow[rows, :width] = key
            plow[rows, width:] = value
            gmem[rows, :] = (mul_nt(key, kw[...]) + mul_nt(value, vw[...])).astype(BF16)
            return carried

        lax.fori_loop(0, blocks, finish, 0)
        outs = [
            cp.start(a, b)
            for a, b in (
                (gmem, grad_memory), (res, result), (hid, hidden), (bra, branch), (gbef, grad_before),
                (fin, ffn_in), (gfirst, grad_first), (plow, pairs_low), (cro, crossed), (gcro, grad_cross),
                (flow, first_low), (gqry, grad_query),
            )
        ]
        for c in outs:
            c.wait()


def run_middle(side, lengths, tokens, halting, cotangent, first_sum, memory_in, key_w, value_w, cross_w, mix_w, expand_w, expand_b, contract_w, contract_b, gains, shifts, memory):
    n, d = tokens.shape
    ff = expand_w.shape[1]
    pairs, nk = d // 128, n // KEYS
    V = pltpu.VMEM
    return call(
        middle_kernel,
        [SMEM, SMEM, ANY, VMEM, ANY, ANY, ANY, ANY, ANY, ANY, ANY, ANY, VMEM, ANY, VMEM, VMEM, VMEM, ANY],
        [
            (shape((n, d), F32), ANY),
            (shape((n, ff), BF16), ANY),
            (shape((n, d), BF16), ANY),
            (shape((n, ff), BF16), ANY),
            (shape((n, d), BF16), ANY),
            (shape((n, d), F32), ANY),
            (shape((n, d), BF16), ANY),
            (shape((n, 2 * d), BF16), ANY),
            (shape((n, d), BF16), ANY),
            (shape((n, d), BF16), ANY),
            (shape((n, d), BF16), ANY),
            (shape((n, d), BF16), ANY),
            (shape((SMALL_ROWS, d), F32), VMEM),
        ],
        [
            V((n, d), BF16), V((d, d), BF16), V((d, d), BF16), V((d, d), BF16), V((d, d), BF16),
            V((d, ff), BF16), V((ff, d), BF16), V((n, d), BF16), V((n, d), F32), V((n, d), F32),
            V((pairs, nk, 2 * KEYS, 128), BF16), V((pairs, nk, 128, 2 * KEYS), BF16),
            V((pairs, nk, 2 * KEYS, 128), BF16), V((pairs, nk, 128, 2 * KEYS), BF16),
            V((ROWS, ff), F32), V((d, ROWS), F32), V((HEADS, ROWS), F32), V((HEADS, ROWS), F32), V((d, ROWS), F32),
            V((n, d), F32), V((n, d), F32), V((n, d), F32), V((n, ff), BF16), V((n, d), BF16), V((n, ff), BF16),
            V((n, d), BF16), V((n, d), F32), V((n, d), BF16), V((n, 2 * d), BF16), V((n, d), BF16),
            V((n, d), BF16), V((n, d), BF16), V((n, d), BF16),
            pltpu.SemaphoreType.DMA((24,)),
        ],
        24_000_000_000, 40_000_000, aliases={17: 0}, name="target_middle",
    )(side, lengths, tokens, halting, cotangent, first_sum, memory_in, key_w, value_w, cross_w, mix_w, expand_w, expand_b, contract_w, contract_b, gains, shifts, memory)


def source_back_kernel(
    side_ref, tokens, halting, cotangent, first_sum, grad_memory,
    expand_w, expand_b, contract_w, contract_b, gains, shifts,
    hidden_in, branch_in, before_in, ffn_in_in, first_in, small_in,
    hidden, branch, grad_before, ffn_in, grad_first, small, grad_direct,
    gmem, w1, w2, tok, cot, fsum, slopes, hid, bra, gbef, fin, gfirst, gdir, sems,
):
    side = side_ref[0]
    n, width = tok.shape
    blocks = n // ROWS

    small[...] = small_in[...]

    @pl.when(side == 0)
    def _():
        cp = Copies(sems)
        ins = [
            cp.start(a, b)
            for a, b in (
                (first_sum, fsum), (expand_w, w1), (contract_w, w2), (tokens, tok), (cotangent, cot),
                (grad_memory, gmem),
            )
        ]
        small[...] = jnp.zeros_like(small)
        for c in ins:
            c.wait()
        weights = (w1, expand_b, w2, contract_b)

        def one(i, carried):
            rows = block_rows(i)
            first = norm_parts(fsum[rows, :])[0] * gains[0:1, :] + shifts[0:1, :]
            low = first.astype(BF16)
            fin[rows, :] = low

            def keep_hidden(part, value):
                hid[rows, part] = value

            def keep_before(part, value):
                gbef[rows, part] = value

            unit1, rate1 = norm_parts(ffn_forward_kept(low, first, weights, keep_hidden, slopes))
            state = tok[rows, :].astype(F32)
            running = column(halting[:, block_rows(i)].astype(F32))
            unit2, rate2 = norm_parts(
                state + running * (unit1 * gains[1:2, :] + shifts[1:2, :] - state)
            )
            grad = cot[rows, :] + gmem[rows, :].astype(F32)
            small[2:3, :] += colsum(grad * unit2)
            small[5:6, :] += colsum(grad)
            grad = norm_back(grad, unit2, rate2, gains[2:3, :])
            gdir[rows, :] = (1.0 - running) * grad
            grad = running * grad
            small[1:2, :] += colsum(grad * unit1)
            small[4:5, :] += colsum(grad)
            grad_low, grad = ffn_back(
                norm_back(grad, unit1, rate1, gains[1:2, :]), weights, slopes, keep_before, small
            )
            bra[rows, :] = grad_low
            small[6:7, :] += colsum(grad_low.astype(F32))
            gfirst[rows, :] = grad
            return carried

        lax.fori_loop(0, blocks, one, 0)
        outs = [
            cp.start(a, b)
            for a, b in (
                (hid, hidden), (bra, branch), (gbef, grad_before), (fin, ffn_in), (gfirst, grad_first),
                (gdir, grad_direct),
            )
        ]
        for c in outs:
            c.wait()


def run_source_back(side, tokens, halting, cotangent, first_sum, grad_memory, expand_w, expand_b, contract_w, contract_b, gains, shifts, hidden, branch, before, ffn_in, first, small):
    n, d = tokens.shape
    ff = expand_w.shape[1]
    V = pltpu.VMEM
    return call(
        source_back_kernel,
        [SMEM, ANY, VMEM, ANY, ANY, ANY, ANY, VMEM, ANY, VMEM, VMEM, VMEM, ANY, ANY, ANY, ANY, ANY, VMEM],
        [
            (shape((n, ff), BF16), ANY), (shape((n, d), BF16), ANY), (shape((n, ff), BF16), ANY),
            (shape((n, d), BF16), ANY), (shape((n, d), F32), ANY), (shape((SMALL_ROWS, d), F32), VMEM),
            (shape((n, d), F32), ANY),
        ],
        [
            V((n, d), BF16), V((d, ff), BF16), V((ff, d), BF16), V((n, d), BF16), V((n, d), F32), V((n, d), F32),
            V((ROWS, ff), F32), V((n, ff), BF16), V((n, d), BF16), V((n, ff), BF16), V((n, d), BF16),
            V((n, d), F32), V((n, d), F32), pltpu.SemaphoreType.DMA((12,)),
        ],
        13_000_000_000, 30_000_000, aliases={12: 0, 13: 1, 14: 2, 15: 3, 16: 4, 17: 5}, name="source_back",
    )(side, tokens, halting, cotangent, first_sum, grad_memory, expand_w, expand_b, contract_w, contract_b, gains, shifts, hidden, branch, before, ffn_in, first, small)


def self_back_kernel(
    side_ref, lengths, halting, cotangent, first_sum, grad_first, grad_direct, projected, attended, logs,
    weight_in, weight_out, gains,
    input_grad, grad_projected, grad_mix, small,
    cot, fsum, gfirst, gdir, proj, att, win, wout, keys, keys_t, values, gqt, gk, gv, gsum, gmix, gproj, ingrad, sems,
):
    side = side_ref[0]
    n, width = cot.shape
    blocks = n // ROWS
    pairs = width // 128
    scale = 1.0 / math.sqrt(width // HEADS)
    cp = Copies(sems)
    c_proj = cp.start(projected, proj)
    ins = [
        cp.start(a, b)
        for a, b in (
            (first_sum, fsum), (grad_first, gfirst), (weight_out, wout), (attended, att),
            (cotangent, cot), (grad_direct, gdir), (weight_in, win),
        )
    ]
    small[...] = jnp.zeros_like(small)
    gk[...] = jnp.zeros_like(gk)
    gv[...] = jnp.zeros_like(gv)
    c_proj.wait()

    def prepare(i, carried):
        rows = block_rows(i)
        split_heads((proj[rows, width : 2 * width], 2 * i), keys, pairs)
        split_heads_turned((proj[rows, width : 2 * width], 2 * i), keys_t, pairs)
        split_heads((proj[rows, 2 * width :], 2 * i), values, pairs)
        return carried

    lax.fori_loop(0, blocks, prepare, 0)
    for c in ins:
        c.wait()

    def one(i, carried):
        rows = block_rows(i)
        unit, rate = norm_parts(fsum[rows, :])
        grad = gfirst[rows, :]
        small[0:1, :] += colsum(grad * unit)
        small[3:4, :] += colsum(grad)
        grad = norm_back(grad, unit, rate, gains[0:1, :])
        gsum[rows, :] = grad
        grad_low = grad.astype(BF16)
        gmix[rows, :] = grad_low
        grad_att = mul_nt(grad_low, wout[...]).astype(BF16)
        queries = proj[rows, :width] * BF16(scale)
        span = bounds(lengths, side, side, i, side == 1)
        attend_block_back(
            queries, grad_att, keys, keys_t, values, span, logs[i], row_inner(grad_att, att[rows, :]), gqt, gk, gv
        )
        gproj[rows, :width] = (gqt[...] * scale).astype(BF16).T
        return carried

    lax.fori_loop(0, blocks, one, 0)

    def finish(i, carried):
        rows = block_rows(i)
        gproj[rows, width : 2 * width] = gk[rows, :].astype(BF16)
        gproj[rows, 2 * width :] = gv[rows, :].astype(BF16)
        ingrad[rows, :] = gsum[rows, :] + mul_nt(gproj[rows, :], win[...])

        @pl.when(side == 0)
        def _():
            ingrad[rows, :] += gdir[rows, :]

        @pl.when(side == 1)
        def _():
            running = column(halting[:, block_rows(i)].astype(F32))
            ingrad[rows, :] += (1.0 - running) * cot[rows, :]

        return carried

    lax.fori_loop(0, blocks, finish, 0)
    outs = [
        cp.start(a, b) for a, b in ((ingrad, input_grad), (gproj, grad_projected), (gmix, grad_mix))
    ]
    for c in outs:
        c.wait()


def run_self_back(side, lengths, halting, cotangent, first_sum, grad_first, grad_direct, projected, attended, logs, weight_in, weight_out, gains):
    n, d = cotangent.shape
    pairs, nk = d // 128, n // KEYS
    V = pltpu.VMEM
    return call(
        self_back_kernel,
        [SMEM, SMEM, VMEM, ANY, ANY, ANY, ANY, ANY, ANY, VMEM, ANY, ANY, VMEM],
        [
            (shape((n, d), F32), ANY), (shape((n, 3 * d), BF16), ANY), (shape((n, d), BF16), ANY),
            (shape((SMALL_ROWS, d), F32), VMEM),
        ],
        [
            V((n, d), F32), V((n, d), F32), V((n, d), F32), V((n, d), F32), V((n, 3 * d), BF16), V((n, d), BF16),
            V((d, 3 * d), BF16), V((d, d), BF16),
            V((pairs, nk, 2 * KEYS, 128), BF16), V((pairs, nk, 128, 2 * KEYS), BF16), V((pairs, nk, 2 * KEYS, 128), BF16),
            V((d, ROWS), F32), V((n, d), F32), V((n, d), F32), V((n, d), F32), V((n, d), BF16), V((n, 3 * d), BF16),
            V((n, d), F32), pltpu.SemaphoreType.DMA((12,)),
        ],
        16_000_000_000, 30_000_000, name="self_back",
    )(side, lengths, halting, cotangent, first_sum, grad_first, grad_direct, projected, attended, logs, weight_in, weight_out, gains)


def exchange(mine, bit, axis):
    count = lax.axis_size(axis)
    return lax.ppermute(mine, axis, [(i, i ^ bit) for i in range(count)])


def take(parts, index):
    return lax.dynamic_index_in_dim(parts, index, 0, keepdims=False)


def halve(value, bit, axis):
    own = (lax.axis_index(axis) // bit) % 2
    parts = value.reshape((2, value.shape[0] // 2) + value.shape[1:])
    came = exchange(take(parts, 1 - own), bit, axis)
    return (take(parts, own).astype(F32) + came.astype(F32)).astype(BF16)


def double(value, bit, axis):
    own = (lax.axis_index(axis) // bit) % 2
    came = exchange(value, bit, axis)
    low = jnp.where(own == 0, value, came)
    high = jnp.where(own == 0, came, value)
    return jnp.concatenate([low, high], axis=0)


def sum_over(value, axis):
    bits = []
    bit = 1
    while bit < lax.axis_size(axis):
        bits.append(bit)
        bit *= 2
    for bit in bits:
        value = halve(value, bit, axis)
    for bit in reversed(bits):
        value = double(value, bit, axis)
    return value


def mul_tn(left, right):
    return lax.dot_general(left, right, (((0,), (0,)), ((), ())), preferred_element_type=F32)


def body(
    tokens, cotangent, lengths, halting, attention_in, attention_out, cross_first, cross_second,
    expand_weight, expand_bias, contract_weight, contract_bias, norm_gain, norm_bias,
):
    side_index = lax.axis_index("half")
    side = side_index.astype(jnp.int32).reshape((1,))
    tok, cot = tokens[0, 0], cotangent[0, 0]
    lens = lengths[:, 0]
    halt = halting[0]
    w_in, w_out, w_one, w_two = attention_in[0], attention_out[0], cross_first[0], cross_second[0]
    w1, w2 = expand_weight[0], contract_weight[0]
    gains, shifts = norm_gain[0], norm_bias[0]
    n, d = tok.shape
    ff = w1.shape[1]
    there, back = [(0, 1)], [(1, 0)]
    source_pair = lax.ppermute(jnp.concatenate([w_one, w_two], axis=0), "half", there)
    start_low, projected, attended, logs, first_sum, memory, memory_low = run_first(
        side, lens, tok, halt, w_in, w_out, w1, expand_bias, w2, contract_bias, w_one, w_two, gains, shifts
    )
    memory_in = lax.ppermute(memory_low, "half", there)
    (
        result, hidden, branch, grad_before, ffn_in, grad_first, grad_memory,
        pairs_low, crossed, grad_cross, first_low, grad_query, small_one,
    ) = run_middle(
        side, lens, tok, halt, cot, first_sum, memory_in, source_pair[:d], source_pair[d:], w_one, w_two,
        w1, expand_bias, w2, contract_bias, gains, shifts, memory,
    )
    grad_in = lax.ppermute(grad_memory, "half", back)
    hidden, branch, grad_before, ffn_in, grad_first, small_one, grad_direct = run_source_back(
        side, tok, halt, cot, first_sum, grad_in, w1, expand_bias, w2, contract_bias, gains, shifts,
        hidden, branch, grad_before, ffn_in, grad_first, small_one,
    )

    def cross_grads():
        return jnp.concatenate(
            [
                mul_tn(first_low, grad_query).astype(BF16),
                mul_tn(crossed, grad_cross).astype(BF16),
                mul_tn(memory_in, pairs_low[:, :d]).astype(BF16),
                mul_tn(memory_in, pairs_low[:, d:]).astype(BF16),
            ],
            axis=0,
        )

    cross = lax.cond(side_index == 1, cross_grads, lambda: jnp.zeros((4 * d, d), BF16))
    ffn = jnp.concatenate(
        [mul_tn(hidden, branch).astype(BF16), mul_tn(grad_before, ffn_in).astype(BF16)], axis=0
    )
    input_grad, grad_projected, grad_mix, small_two = run_self_back(
        side, lens, halt, cot, first_sum, grad_first, grad_direct, projected, attended, logs, w_in, w_out, gains
    )
    attn = jnp.concatenate(
        [
            mul_tn(grad_projected, start_low).astype(BF16),
            mul_tn(attended, grad_mix).astype(BF16),
            (small_one + small_two).astype(BF16),
        ],
        axis=0,
    )
    attn = jnp.concatenate([attn, jnp.zeros((-attn.shape[0] % 1024, d), BF16)], axis=0)
    cross = sum_over(cross, "dp")
    ffn = sum_over(ffn, "dp")
    attn = sum_over(attn, "dp")
    from_target = lax.ppermute(cross[2 * d :], "half", back)
    cross = jnp.where(side_index == 1, cross[: 2 * d], from_target).astype(F32)
    small = attn[4 * d : 4 * d + SMALL_ROWS].astype(F32)
    return (
        result[None, None],
        input_grad[None, None],
        attn[: 3 * d].astype(F32).T[None],
        attn[3 * d : 4 * d].astype(F32)[None],
        cross[:d][None],
        cross[d:][None],
        ffn[ff:].astype(F32).T[None],
        small[8 : 8 + ff // d].reshape(1, ff),
        ffn[:ff].astype(F32)[None],
        small[6:7],
        small[0:3][None],
        small[3:6][None],
    )


def solution(mesh):
    placed = (
        P("half", "dp", None, None),
        P("half", "dp", None, None),
        P(None, "dp", None),
        P("half", "dp", None),
        P("half", None, None),
        P("half", None, None),
        P("half", None, None),
        P("half", None, None),
        P("half", None, None),
        P("half", None),
        P("half", None, None),
        P("half", None),
        P("half", None, None),
        P("half", None, None),
    )
    return jax.shard_map(
        body,
        mesh=mesh,
        in_specs=placed,
        out_specs=(
            P("half", "dp", None, None),
            P("half", "dp", None, None),
            P("half", None, None),
            P("half", None, None),
            P("half", None, None),
            P("half", None, None),
            P("half", None, None),
            P("half", None),
            P("half", None, None),
            P("half", None),
            P("half", None, None),
            P("half", None, None),
        ),
        check_vma=False,
    )
```

```python
from functools import partial
import math

import jax
import jax.numpy as jnp
from jax import lax
from jax.experimental import pallas as pl
from jax.experimental.pallas import tpu as pltpu
from jax.sharding import PartitionSpec as P

HEADS = 8
STEP = 2
EPSILON = 1e-06
LONGEST = 256
ROWS = 256
KEYS = 128
PIECE = 512
MASKED = -1e30
VMEM_BYTES = 60 * 1024 * 1024
F32 = jnp.float32
BF16 = jnp.bfloat16


def mul(left, right):
    return jnp.dot(left, right, preferred_element_type=F32)


def mul_nt(left, right):
    return lax.dot_general(left, right, (((1,), (1,)), ((), ())), preferred_element_type=F32)


def iota(shape, axis):
    return lax.broadcasted_iota(jnp.int32, shape, axis)


def norm_parts(summed):
    center = summed - jnp.mean(summed, axis=-1, keepdims=True)
    rate = lax.rsqrt(jnp.mean(center * center, axis=-1, keepdims=True) + EPSILON)
    return center * rate, rate


def norm_back(grad, unit, rate, gain):
    scaled = grad * gain
    return rate * (
        scaled
        - jnp.mean(scaled, axis=-1, keepdims=True)
        - unit * jnp.mean(scaled * unit, axis=-1, keepdims=True)
    )


def gate(before):
    inner = math.sqrt(2.0 / math.pi) * (before + 0.044715 * before * before * before)
    half_one = 0.5 * (1.0 + jnp.tanh(inner))
    return before * half_one


def gate_and_slope(before):
    scale = math.sqrt(2.0 / math.pi)
    square = before * before
    bent = jnp.tanh(scale * before * (1.0 + 0.044715 * square))
    half_one = 0.5 + 0.5 * bent
    slope = half_one + 0.5 * before * (1.0 - bent * bent) * (
        scale * (1.0 + 3 * 0.044715 * square)
    )
    return before * half_one, slope


def bounds(lengths, side, key_side, block, causal):
    first_row = block * ROWS
    last_row = first_row + ROWS - 1
    place = first_row + iota((1, ROWS), 1)
    low = jnp.zeros((1, ROWS), jnp.int32)
    high = jnp.zeros((1, ROWS), jnp.int32)
    least = jnp.int32(0)
    most = jnp.int32(0)
    at = jnp.int32(0)
    key_at = jnp.int32(0)
    for k in range(lengths.shape[1]):
        end = at + lengths[side, k]
        key_end = key_at + lengths[key_side, k]
        inside = (place >= at) & (place < end)
        low = jnp.where(inside, key_at, low)
        high = jnp.where(inside, key_end, high)
        least = jnp.where((first_row >= at) & (first_row < end), key_at, least)
        most = jnp.where((last_row >= at) & (last_row < end), key_end, most)
        at, key_at = end, key_end
    if causal is not None:
        high = jnp.where(causal, jnp.minimum(high, place + 1), high)
        most = jnp.where(causal, jnp.minimum(most, last_row + 1), most)
    return low, high, least // KEYS, (most + KEYS - 1) // KEYS


def keep_pair(block, axis):
    place = iota(block.shape, axis)
    half = block.shape[axis] // 2
    zero = jnp.zeros_like(block)
    return jnp.concatenate(
        [jnp.where(place < half, block, zero), jnp.where(place >= half, block, zero)],
        axis=1 - axis,
    )


def split_heads(source, stacked, pairs):
    block, base = source
    for p in range(pairs):
        for t in range(ROWS // KEYS):
            part = block[t * KEYS : (t + 1) * KEYS, p * 128 : (p + 1) * 128]
            stacked[p, base + t] = keep_pair(part, 1)


def split_heads_turned(source, stacked, pairs):
    block, base = source
    turned = block.T
    for p in range(pairs):
        for t in range(ROWS // KEYS):
            part = turned[p * 128 : (p + 1) * 128, t * KEYS : (t + 1) * KEYS]
            stacked[p, base + t] = keep_pair(part, 0)


def mask_bias(block_index, low, high):
    key_place = block_index * KEYS + iota((KEYS, ROWS), 0)
    return jnp.where((key_place >= low) & (key_place < high), 0.0, MASKED)


def attend_block(queries, keys, values_turned, span, mixed, top, total):
    low, high, least, most = span
    pairs = keys.shape[0]
    mixed[...] = jnp.zeros_like(mixed)
    top[...] = jnp.full(top.shape, MASKED, F32)
    total[...] = jnp.zeros_like(total)

    def one(j, carried):
        bias = mask_bias(j, low, high)
        old = top[...]
        scores = [mul_nt(keys[p, j], queries[:, p * 128 : (p + 1) * 128]) for p in range(pairs)]
        parts = [scores[h // 2][(h % 2) * KEYS : (h % 2 + 1) * KEYS] + bias for h in range(2 * pairs)]
        new = jnp.maximum(old, jnp.concatenate([jnp.max(t, axis=0, keepdims=True) for t in parts], axis=0))
        fade = jnp.exp(old - new)
        weights = [jnp.exp(t - new[h : h + 1]) for h, t in enumerate(parts)]
        total[...] = total[...] * fade + jnp.concatenate(
            [jnp.sum(w, axis=0, keepdims=True) for w in weights], axis=0
        )
        top[...] = new
        for p in range(pairs):
            pair = jnp.concatenate([weights[2 * p].astype(BF16), weights[2 * p + 1].astype(BF16)], axis=0)
            added = mul(values_turned[p, j], pair)
            for u in range(2):
                at = p * 128 + u * 64
                mixed[at : at + 64, :] = (
                    mixed[at : at + 64, :] * fade[2 * p + u : 2 * p + u + 1] + added[u * 64 : (u + 1) * 64]
                )
        return carried

    lax.fori_loop(least, most, one, 0)
    for h in range(2 * pairs):
        rate = 1.0 / total[h : h + 1, :]
        mixed[h * 64 : (h + 1) * 64, :] = mixed[h * 64 : (h + 1) * 64, :] * rate
    top[...] = top[...] + jnp.log(total[...])


def attend_block_back(
    queries, grads, keys, keys_turned, values, span, logs, inner, grad_queries, grad_keys, grad_values
):
    low, high, least, most = span
    pairs = keys.shape[0]
    grad_queries[...] = jnp.zeros_like(grad_queries)
    first_half = iota((KEYS, 128), 1) < 64

    def one(j, carried):
        bias = mask_bias(j, low, high)
        rows = pl.ds(pl.multiple_of(j * KEYS, KEYS), KEYS)
        lanes = [slice(p * 128, (p + 1) * 128) for p in range(pairs)]
        scores = [mul_nt(keys[p, j], queries[:, lanes[p]]) for p in range(pairs)]
        grad_probs = [mul_nt(values[p, j], grads[:, lanes[p]]) for p in range(pairs)]
        probs, grad_scores = [], []
        for h in range(2 * pairs):
            part = slice((h % 2) * KEYS, (h % 2 + 1) * KEYS)
            prob = jnp.exp(scores[h // 2][part] + bias - logs[h : h + 1, :])
            probs.append(prob.astype(BF16))
            grad_scores.append((prob * (grad_probs[h // 2][part] - inner[h : h + 1, :])).astype(BF16))
        for p in range(pairs):
            both = mul(jnp.concatenate(probs[2 * p : 2 * p + 2], axis=0), grads[:, lanes[p]])
            grad_values[rows, lanes[p]] += jnp.where(first_half, both[:KEYS], both[KEYS:])
        for p in range(pairs):
            grad_pair = jnp.concatenate(grad_scores[2 * p : 2 * p + 2], axis=0)
            both = mul(grad_pair, queries[:, lanes[p]])
            grad_keys[rows, lanes[p]] += jnp.where(first_half, both[:KEYS], both[KEYS:])
            grad_queries[lanes[p], :] += mul(keys_turned[p, j], grad_pair)
        return carried

    lax.fori_loop(least, most, one, 0)


def row_inner(grads, mixed):
    width = grads.shape[1]
    head_of = iota((16, width), 1) // (width // HEADS)
    picks = (head_of == iota((16, width), 0)).astype(BF16)
    product = grads.astype(F32) * mixed.astype(F32)
    big = product.astype(BF16)
    small = (product - big.astype(F32)).astype(BF16)
    return mul_nt(picks, big) + mul_nt(picks, small)


def column(row):
    return jnp.broadcast_to(row, (128, row.shape[1])).T[:, :1]


class Copies:
    def __init__(self, sems):
        self.sems = sems
        self.used = 0

    def start(self, source, target):
        copy = pltpu.make_async_copy(source, target, self.sems.at[self.used])
        self.used += 1
        copy.start()
        return copy


def block_rows(i):
    return pl.ds(pl.multiple_of(i * ROWS, ROWS), ROWS)


class RowCopies:
    def __init__(self, pairs, sems, blocks):
        self.pairs, self.sems, self.blocks = pairs, sems, blocks

    def copy(self, k, i):
        source, target = self.pairs[k]
        rows = block_rows(i)
        return pltpu.make_async_copy(source.at[rows, :], target.at[rows, :], self.sems.at[k, i])

    def start(self, i):
        for k in range(len(self.pairs)):
            self.copy(k, i).start()

    def wait(self):
        for i in range(self.blocks):
            for k in range(len(self.pairs)):
                self.copy(k, i).wait()


def colsum(values):
    return jnp.sum(values, axis=0, keepdims=True)


def ffn_forward(low_in, base, weights):
    expand_w, expand_b, contract_w, contract_b = weights
    total = base + contract_b[...]
    for c in range(expand_w.shape[1] // PIECE):
        part = slice(c * PIECE, (c + 1) * PIECE)
        before = mul(low_in, expand_w[:, part]) + expand_b[:, part]
        total = total + mul(gate(before).astype(BF16), contract_w[part, :])
    return total


def ffn_forward_kept(low_in, base, weights, hidden, slopes):
    expand_w, expand_b, contract_w, contract_b = weights
    total = base + contract_b[...]
    for c in range(expand_w.shape[1] // PIECE):
        part = slice(c * PIECE, (c + 1) * PIECE)
        before = mul(low_in, expand_w[:, part]) + expand_b[:, part]
        gated, slope = gate_and_slope(before)
        gated = gated.astype(BF16)
        hidden(part, gated)
        slopes[:, part] = slope
        total = total + mul(gated, contract_w[part, :])
    return total


def ffn_back(grad_summed, weights, slopes, grad_before, small):
    expand_w, _, contract_w, _ = weights
    branch = grad_summed.astype(BF16)
    grad_in = grad_summed
    for c in range(expand_w.shape[1] // PIECE):
        part = slice(c * PIECE, (c + 1) * PIECE)
        pushed = (mul_nt(branch, contract_w[part, :]) * slopes[:, part]).astype(BF16)
        grad_before(part, pushed)
        small[8 + c : 9 + c, :] += colsum(pushed.astype(F32))
        grad_in = grad_in + mul_nt(pushed, expand_w[:, part])
    return branch, grad_in


def first_kernel(
    side_ref, lengths, tokens, halting, weight_in, weight_out, expand_w, expand_b, contract_w,
    contract_b, cross_w, value_w, gains, shifts,
    start_low, projected, attended, logs, first_sum, memory, memory_low,
    tok, win, wout, w1, w2, table_big, table_small, start, proj, keys, values_turned, mixed, top, total,
    att, fsum, mem, meml, slow, sems, early_sems, late_sems, source_sems,
):
    side = side_ref[0]
    blocks = tokens.shape[0] // ROWS
    early = RowCopies([(slow, start_low), (proj, projected)], early_sems, blocks)
    late = RowCopies([(att, attended), (fsum, first_sum)], late_sems, blocks)
    source = RowCopies([(mem, memory), (meml, memory_low)], source_sems, blocks)
    width = tokens.shape[1]
    pairs = width // 128
    cp = Copies(sems)
    c_tok = cp.start(tokens, tok)
    c_in = cp.start(weight_in, win)
    c_out = cp.start(weight_out, wout)
    c_w1 = cp.start(expand_w, w1)
    c_w2 = cp.start(contract_w, w2)

    half = width // 2
    rate = jnp.exp(iota((16, half), 1).astype(F32) * (-math.log(10000.0) / half))
    fine = iota((16, half), 0).astype(F32) * rate
    coarse = fine * 16.0
    fine_s, fine_c, coarse_s, coarse_c = jnp.sin(fine), jnp.cos(fine), jnp.sin(coarse), jnp.cos(coarse)
    step_s, step_c = fine_s[STEP : STEP + 1], fine_c[STEP : STEP + 1]
    for a in range(LONGEST // 16):
        s, c = coarse_s[a : a + 1], coarse_c[a : a + 1]
        whole = jnp.concatenate(
            [s * fine_c + c * fine_s + step_s, c * fine_c - s * fine_s + step_c], axis=1
        )
        big = whole.astype(BF16)
        table_big[a * 16 : (a + 1) * 16, :] = big
        table_small[a * 16 : (a + 1) * 16, :] = (whole - big.astype(F32)).astype(BF16)

    lane = iota((1, 128), 1)
    begins = jnp.zeros((1, 128), jnp.int32)
    at = jnp.int32(0)
    for k in range(lengths.shape[1]):
        begins = jnp.where(lane == k, at, begins)
        at = at + lengths[side, k]
    c_tok.wait()
    c_in.wait()

    def prepare(i, carried):
        rows = block_rows(i)
        place = i * ROWS + iota((ROWS, 1), 0)
        began = jnp.max(jnp.where(place >= begins, begins, 0), axis=1, keepdims=True)
        picks = (iota((ROWS, LONGEST), 1) == place - began).astype(F32).astype(BF16)
        block = tok[rows, :].astype(F32) + (mul(picks, table_big[...]) + mul(picks, table_small[...]))
        start[rows, :] = block
        low = block.astype(BF16)
        slow[rows, :] = low
        sent = mul(low, win[...]).astype(BF16)
        proj[rows, :] = sent
        split_heads((sent[:, width : 2 * width], 2 * i), keys, pairs)
        split_heads_turned((sent[:, 2 * width :], 2 * i), values_turned, pairs)
        early.start(i)
        return carried

    lax.fori_loop(0, blocks, prepare, 0)
    c_out.wait()
    c_w1.wait()
    c_w2.wait()
    weights = (w1, expand_b, w2, contract_b)

    def attend(i, carried):
        rows = block_rows(i)
        queries = proj[rows, :width] * BF16(1.0 / math.sqrt(width // HEADS))
        attend_block(
            queries, keys, values_turned, bounds(lengths, side, side, i, side == 1), mixed, top, total
        )
        logs[i] = top[...]
        low = mixed[...].astype(BF16).T
        att[rows, :] = low
        summed = start[rows, :] + mul(low, wout[...])
        fsum[rows, :] = summed

        @pl.when(side == 0)
        def _():
            first = norm_parts(summed)[0] * gains[0:1, :] + shifts[0:1, :]
            tail = norm_parts(ffn_forward(first.astype(BF16), first, weights))[0] * gains[1:2, :] + shifts[1:2, :]
            state = tok[rows, :].astype(F32)
            running = column(halting[:, block_rows(i)].astype(F32))
            stepped = state + running * (tail - state)
            kept = norm_parts(stepped)[0] * gains[2:3, :] + shifts[2:3, :]
            mem[rows, :] = kept
            meml[rows, :] = kept.astype(BF16)
            source.start(i)

        late.start(i)
        return carried

    lax.fori_loop(0, blocks, attend, 0)
    early.wait()
    late.wait()

    @pl.when(side == 0)
    def _():
        source.wait()


ANY = pl.BlockSpec(memory_space=pl.ANY)
SMEM = pl.BlockSpec(memory_space=pltpu.SMEM)
VMEM = pl.BlockSpec(memory_space=pltpu.VMEM)


def shape(s, d):
    return jax.ShapeDtypeStruct(s, d)


def call(kernel, ins, outs, scratch, flops, moved, aliases=None, name=None):
    return pl.pallas_call(
        kernel,
        in_specs=ins,
        out_specs=[o[1] for o in outs],
        out_shape=[o[0] for o in outs],
        scratch_shapes=scratch,
        input_output_aliases=aliases or {},
        compiler_params=pltpu.CompilerParams(vmem_limit_bytes=VMEM_BYTES),
        cost_estimate=pl.CostEstimate(flops=flops, bytes_accessed=moved, transcendentals=0),
        name=name,
    )


def run_first(side, lengths, tokens, halting, weight_in, weight_out, expand_w, expand_b, contract_w, contract_b, cross_w, value_w, gains, shifts):
    n, d = tokens.shape
    ff = expand_w.shape[1]
    pairs, nk = d // 128, n // KEYS
    V = pltpu.VMEM
    return call(
        first_kernel,
        [SMEM, SMEM, ANY, VMEM, ANY, ANY, ANY, VMEM, ANY, VMEM, ANY, ANY, VMEM, VMEM],
        [
            (shape((n, d), BF16), ANY),
            (shape((n, 3 * d), BF16), ANY),
            (shape((n, d), BF16), ANY),
            (shape((n // ROWS, HEADS, ROWS), F32), VMEM),
            (shape((n, d), F32), ANY),
            (shape((n, d), F32), ANY),
            (shape((n, d), BF16), ANY),
        ],
        [
            V((n, d), BF16), V((d, 3 * d), BF16), V((d, d), BF16), V((d, ff), BF16), V((ff, d), BF16),
            V((LONGEST, d), BF16), V((LONGEST, d), BF16), V((n, d), F32), V((n, 3 * d), BF16),
            V((pairs, nk, 2 * KEYS, 128), BF16), V((pairs, nk, 128, 2 * KEYS), BF16),
            V((d, ROWS), F32), V((HEADS, ROWS), F32), V((HEADS, ROWS), F32),
            V((n, d), BF16), V((n, d), F32), V((n, d), F32), V((n, d), BF16), V((n, d), BF16),
            pltpu.SemaphoreType.DMA((5,)), pltpu.SemaphoreType.DMA((2, n // ROWS)),
            pltpu.SemaphoreType.DMA((2, n // ROWS)), pltpu.SemaphoreType.DMA((2, n // ROWS)),
        ],
        12_000_000_000, 20_000_000, name="first_part",
    )(side, lengths, tokens, halting, weight_in, weight_out, expand_w, expand_b, contract_w, contract_b, cross_w, value_w, gains, shifts)


SMALL_ROWS = 16


def middle_kernel(
    side_ref, lengths, tokens, halting, cotangent, first_sum, memory_in, key_w, value_w, cross_w, mix_w,
    expand_w, expand_b, contract_w, contract_b, gains, shifts, memory,
    result, hidden, branch, grad_before, ffn_in, grad_first, grad_memory,
    pairs_low, crossed, grad_cross, first_low, grad_query, kept, small,
    mlow, kw, vw, cw, mw, w1, w2, tok, cot, fsum, keys, keys_t, values, values_t, slopes,
    mixed, top, total, gqt, gk, gv, res, hid, bra, gbef, fin, gfirst, gmem, plow, cro, gcro, flow, gqry, sems, out_sems, source_sems,
):
    side = side_ref[0]
    n, width = tok.shape
    blocks = n // ROWS
    pairs = width // 128
    scale = 1.0 / math.sqrt(width // HEADS)

    @pl.when(side == 0)
    def _():
        cp = Copies(sems)
        ins = [
            cp.start(a, b) for a, b in ((first_sum, fsum), (tokens, tok), (expand_w, w1), (contract_w, w2))
        ]
        outs = RowCopies(
            [(hid, hidden), (gbef, grad_before), (fin, ffn_in), (gfirst, grad_first), (res, kept)], source_sems, blocks
        )
        small[...] = jnp.zeros_like(small)
        for c in ins:
            c.wait()
        weights = (w1, expand_b, w2, contract_b)

        def one(i, carried):
            rows = block_rows(i)
            first = norm_parts(fsum[rows, :])[0] * gains[0:1, :] + shifts[0:1, :]
            low = first.astype(BF16)
            fin[rows, :] = low

            def keep_hidden(part, value):
                hid[rows, part] = value

            summed = ffn_forward_kept(low, first, weights, keep_hidden, slopes)
            gbef[rows, :] = slopes[...].astype(BF16)
            res[rows, :] = summed
            tail = norm_parts(summed)[0] * gains[1:2, :] + shifts[1:2, :]
            state = tok[rows, :].astype(F32)
            running = column(halting[:, block_rows(i)].astype(F32))
            gfirst[rows, :] = state + running * (tail - state)
            outs.start(i)
            return carried

        lax.fori_loop(0, blocks, one, 0)
        outs.wait()

    @pl.when(side == 1)
    def _():
        cp = Copies(sems)
        c_mlow = cp.start(memory_in, mlow)
        c_kw, c_vw = cp.start(key_w, kw), cp.start(value_w, vw)
        rest = [
            cp.start(a, b)
            for a, b in (
                (cross_w, cw), (mix_w, mw), (first_sum, fsum), (expand_w, w1), (contract_w, w2),
                (tokens, tok), (cotangent, cot),
            )
        ]
        outs = RowCopies(
            [
                (res, result), (hid, hidden), (bra, branch), (gbef, grad_before), (fin, ffn_in),
                (gfirst, grad_first), (cro, crossed), (gcro, grad_cross), (flow, first_low), (gqry, grad_query),
            ],
            out_sems, blocks,
        )
        last = RowCopies([(gmem, grad_memory), (plow, pairs_low)], source_sems, blocks)
        small[...] = jnp.zeros_like(small)
        gk[...] = jnp.zeros_like(gk)
        gv[...] = jnp.zeros_like(gv)
        c_mlow.wait()
        c_kw.wait()
        c_vw.wait()

        def prepare(i, carried):
            low = mlow[block_rows(i), :]
            key = mul(low, kw[...]).astype(BF16)
            value = mul(low, vw[...]).astype(BF16)
            split_heads((key, 2 * i), keys, pairs)
            split_heads((value, 2 * i), values, pairs)
            split_heads_turned((key, 2 * i), keys_t, pairs)
            split_heads_turned((value, 2 * i), values_t, pairs)
            return carried

        lax.fori_loop(0, blocks, prepare, 0)
        for c in rest:
            c.wait()
        weights = (w1, expand_b, w2, contract_b)

        def one(i, carried):
            rows = block_rows(i)
            first = norm_parts(fsum[rows, :])[0] * gains[0:1, :] + shifts[0:1, :]
            low = first.astype(BF16)
            flow[rows, :] = low
            queries = mul(low, cw[...]).astype(BF16) * BF16(scale)
            span = bounds(lengths, 1, 0, i, None)
            attend_block(queries, keys, values_t, span, mixed, top, total)
            mix_low = mixed[...].astype(BF16).T
            cro[rows, :] = mix_low
            unit2, rate2 = norm_parts(first + mul(mix_low, mw[...]))
            second = unit2 * gains[2:3, :] + shifts[2:3, :]
            low = second.astype(BF16)
            fin[rows, :] = low

            def keep_hidden(part, value):
                hid[rows, part] = value

            def keep_before(part, value):
                gbef[rows, part] = value

            unit1, rate1 = norm_parts(ffn_forward_kept(low, second, weights, keep_hidden, slopes))
            state = tok[rows, :].astype(F32)
            running = column(halting[:, block_rows(i)].astype(F32))
            res[rows, :] = state + running * (unit1 * gains[1:2, :] + shifts[1:2, :] - state)
            grad = running * cot[rows, :]
            small[1:2, :] += colsum(grad * unit1)
            small[4:5, :] += colsum(grad)
            grad_low, grad = ffn_back(
                norm_back(grad, unit1, rate1, gains[1:2, :]), weights, slopes, keep_before, small
            )
            bra[rows, :] = grad_low
            small[6:7, :] += colsum(grad_low.astype(F32))
            small[2:3, :] += colsum(grad * unit2)
            small[5:6, :] += colsum(grad)
            grad = norm_back(grad, unit2, rate2, gains[2:3, :])
            grad_low = grad.astype(BF16)
            gcro[rows, :] = grad_low
            grad_mix = mul_nt(grad_low, mw[...]).astype(BF16)
            attend_block_back(
                queries, grad_mix, keys, keys_t, values, span, top, row_inner(grad_mix, mix_low), gqt, gk, gv
            )
            grad_low = (gqt[...] * scale).astype(BF16).T
            gqry[rows, :] = grad_low
            gfirst[rows, :] = grad + mul_nt(grad_low, cw[...])
            outs.start(i)
            return carried

        lax.fori_loop(0, blocks, one, 0)

        def finish(i, carried):
            rows = block_rows(i)
            key = gk[rows, :].astype(BF16)
            value = gv[rows, :].astype(BF16)
            plow[rows, :width] = key
            plow[rows, width:] = value
            gmem[rows, :] = (mul_nt(key, kw[...]) + mul_nt(value, vw[...])).astype(BF16)
            last.start(i)
            return carried

        lax.fori_loop(0, blocks, finish, 0)
        outs.wait()
        last.wait()


def run_middle(side, lengths, tokens, halting, cotangent, first_sum, memory_in, key_w, value_w, cross_w, mix_w, expand_w, expand_b, contract_w, contract_b, gains, shifts, memory):
    n, d = tokens.shape
    ff = expand_w.shape[1]
    pairs, nk = d // 128, n // KEYS
    V = pltpu.VMEM
    return call(
        middle_kernel,
        [SMEM, SMEM, ANY, VMEM, ANY, ANY, ANY, ANY, ANY, ANY, ANY, ANY, VMEM, ANY, VMEM, VMEM, VMEM, ANY],
        [
            (shape((n, d), F32), ANY),
            (shape((n, ff), BF16), ANY),
            (shape((n, d), BF16), ANY),
            (shape((n, ff), BF16), ANY),
            (shape((n, d), BF16), ANY),
            (shape((n, d), F32), ANY),
            (shape((n, d), BF16), ANY),
            (shape((n, 2 * d), BF16), ANY),
            (shape((n, d), BF16), ANY),
            (shape((n, d), BF16), ANY),
            (shape((n, d), BF16), ANY),
            (shape((n, d), BF16), ANY),
            (shape((n, d), F32), ANY),
            (shape((SMALL_ROWS, d), F32), VMEM),
        ],
        [
            V((n, d), BF16), V((d, d), BF16), V((d, d), BF16), V((d, d), BF16), V((d, d), BF16),
            V((d, ff), BF16), V((ff, d), BF16), V((n, d), BF16), V((n, d), F32), V((n, d), F32),
            V((pairs, nk, 2 * KEYS, 128), BF16), V((pairs, nk, 128, 2 * KEYS), BF16),
            V((pairs, nk, 2 * KEYS, 128), BF16), V((pairs, nk, 128, 2 * KEYS), BF16),
            V((ROWS, ff), F32), V((d, ROWS), F32), V((HEADS, ROWS), F32), V((HEADS, ROWS), F32), V((d, ROWS), F32),
            V((n, d), F32), V((n, d), F32), V((n, d), F32), V((n, ff), BF16), V((n, d), BF16), V((n, ff), BF16),
            V((n, d), BF16), V((n, d), F32), V((n, d), BF16), V((n, 2 * d), BF16), V((n, d), BF16),
            V((n, d), BF16), V((n, d), BF16), V((n, d), BF16),
            pltpu.SemaphoreType.DMA((10,)), pltpu.SemaphoreType.DMA((10, n // ROWS)),
            pltpu.SemaphoreType.DMA((5, n // ROWS)),
        ],
        24_000_000_000, 40_000_000, aliases={17: 0}, name="target_middle",
    )(side, lengths, tokens, halting, cotangent, first_sum, memory_in, key_w, value_w, cross_w, mix_w, expand_w, expand_b, contract_w, contract_b, gains, shifts, memory)


def back_kernel(
    side_ref, halting, cotangent, first_sum, grad_memory, kept, attended,
    expand_w, contract_w, weight_out, gains, shifts,
    branch_in, before_in, first_in, small_in,
    branch, grad_before, small, grad_direct, grad_sum, grad_mix, grad_att, inner,
    gmem, w1, w2, wout, cot, fsum, step, sum1, att, bra, slo, gbef, gdir, gsum, gmix, gatt,
    sems, source_sems, out_sems,
):
    side = side_ref[0]
    n, width = fsum.shape
    blocks = n // ROWS
    cp = Copies(sems)
    c_first = cp.start(first_in, step)
    c_sum = cp.start(first_sum, fsum)
    c_att = cp.start(attended, att)
    c_out = cp.start(weight_out, wout)
    small[...] = small_in[...]
    outs = RowCopies([(gsum, grad_sum), (gmix, grad_mix), (gatt, grad_att)], out_sems, blocks)

    def open_block(i, grad):
        rows = block_rows(i)
        unit, rate = norm_parts(fsum[rows, :])
        small[0:1, :] += colsum(grad * unit)
        small[3:4, :] += colsum(grad)
        grad = norm_back(grad, unit, rate, gains[0:1, :])
        gsum[rows, :] = grad
        grad_low = grad.astype(BF16)
        gmix[rows, :] = grad_low
        grad_mixed = mul_nt(grad_low, wout[...]).astype(BF16)
        gatt[rows, :] = grad_mixed
        inner[i] = row_inner(grad_mixed, att[rows, :])
        outs.start(i)

    @pl.when(side == 0)
    def _():
        ins = [
            cp.start(a, b)
            for a, b in (
                (grad_memory, gmem), (cotangent, cot), (kept, sum1), (contract_w, w2), (before_in, slo), (expand_w, w1),
            )
        ]
        source_outs = RowCopies([(bra, branch), (gbef, grad_before), (gdir, grad_direct)], source_sems, blocks)
        for c in [c_first, c_sum, c_att, c_out] + ins:
            c.wait()

        def one(i, carried):
            rows = block_rows(i)
            running = column(halting[:, block_rows(i)].astype(F32))
            unit2, rate2 = norm_parts(step[rows, :])
            grad = cot[rows, :] + gmem[rows, :].astype(F32)
            small[2:3, :] += colsum(grad * unit2)
            small[5:6, :] += colsum(grad)
            grad = norm_back(grad, unit2, rate2, gains[2:3, :])
            gdir[rows, :] = (1.0 - running) * grad
            grad = running * grad
            unit1, rate1 = norm_parts(sum1[rows, :])
            small[1:2, :] += colsum(grad * unit1)
            small[4:5, :] += colsum(grad)
            grad_summed = norm_back(grad, unit1, rate1, gains[1:2, :])
            low = grad_summed.astype(BF16)
            bra[rows, :] = low
            small[6:7, :] += colsum(low.astype(F32))
            grad_in = grad_summed
            for c in range(w1.shape[1] // PIECE):
                part = slice(c * PIECE, (c + 1) * PIECE)
                pushed = (mul_nt(low, w2[part, :]) * slo[rows, part].astype(F32)).astype(BF16)
                gbef[rows, part] = pushed
                small[8 + c : 9 + c, :] += colsum(pushed.astype(F32))
                grad_in = grad_in + mul_nt(pushed, w1[:, part])
            source_outs.start(i)
            open_block(i, grad_in)
            return carried

        lax.fori_loop(0, blocks, one, 0)
        source_outs.wait()

    @pl.when(side == 1)
    def _():
        for c in (c_first, c_sum, c_att, c_out):
            c.wait()

        def one(i, carried):
            open_block(i, step[block_rows(i), :])
            return carried

        lax.fori_loop(0, blocks, one, 0)

    outs.wait()


def run_back(side, halting, cotangent, first_sum, grad_memory, kept, attended, expand_w, contract_w, weight_out, gains, shifts, branch, before, first, small):
    n, d = first_sum.shape
    ff = expand_w.shape[1]
    V = pltpu.VMEM
    sem = pltpu.SemaphoreType.DMA
    blocks = n // ROWS
    return call(
        back_kernel,
        [SMEM, VMEM, ANY, ANY, ANY, ANY, ANY, ANY, ANY, ANY, VMEM, VMEM, ANY, ANY, ANY, VMEM],
        [
            (shape((n, d), BF16), ANY), (shape((n, ff), BF16), ANY), (shape((SMALL_ROWS, d), F32), VMEM),
            (shape((n, d), F32), ANY), (shape((n, d), F32), ANY), (shape((n, d), BF16), ANY), (shape((n, d), BF16), ANY),
            (shape((n // ROWS, 16, ROWS), F32), VMEM),
        ],
        [
            V((n, d), BF16), V((d, ff), BF16), V((ff, d), BF16), V((d, d), BF16), V((n, d), F32), V((n, d), F32),
            V((n, d), F32), V((n, d), F32), V((n, d), BF16), V((n, d), BF16), V((n, ff), BF16), V((n, ff), BF16),
            V((n, d), F32), V((n, d), F32), V((n, d), BF16), V((n, d), BF16),
            sem((10,)), sem((3, blocks)), sem((3, blocks)),
        ],
        8_000_000_000, 30_000_000, aliases={12: 0, 13: 1, 15: 2}, name="norms_back",
    )(side, halting, cotangent, first_sum, grad_memory, kept, attended, expand_w, contract_w, weight_out, gains, shifts, branch, before, first, small)


def self_heads_kernel(
    first_pair, side_ref, lengths, projected, grad_att, logs, inner,
    grad_part,
    que, key, val, gatt, keys, keys_t, values, gqt, gk, gv, gpart, sems,
):
    side = side_ref[0]
    n, part = que.shape
    width = grad_att.shape[1]
    blocks = n // ROWS
    pairs = part // 128
    scale = 1.0 / math.sqrt(width // HEADS)
    cp = Copies(sems)
    at = first_pair * 128
    c_key = cp.start(projected.at[:, width + at : width + at + part], key)
    c_val = cp.start(projected.at[:, 2 * width + at : 2 * width + at + part], val)
    c_que = cp.start(projected.at[:, at : at + part], que)
    c_att = cp.start(grad_att.at[:, at : at + part], gatt)
    gk[...] = jnp.zeros_like(gk)
    gv[...] = jnp.zeros_like(gv)
    c_key.wait()
    c_val.wait()

    def prepare(i, carried):
        rows = block_rows(i)
        split_heads((key[rows, :], 2 * i), keys, pairs)
        split_heads_turned((key[rows, :], 2 * i), keys_t, pairs)
        split_heads((val[rows, :], 2 * i), values, pairs)
        return carried

    lax.fori_loop(0, blocks, prepare, 0)
    c_que.wait()
    c_att.wait()

    def one(i, carried):
        rows = block_rows(i)
        queries = que[rows, :] * BF16(scale)
        span = bounds(lengths, side, side, i, side == 1)
        heads = slice(2 * first_pair, 2 * (first_pair + pairs))
        attend_block_back(
            queries, gatt[rows, :], keys, keys_t, values, span, logs[i][heads], inner[i][heads], gqt, gk, gv
        )
        gpart[rows, :part] = (gqt[...] * scale).astype(BF16).T
        return carried

    lax.fori_loop(0, blocks, one, 0)
    gpart[:, part : 2 * part] = gk[...].astype(BF16)
    gpart[:, 2 * part :] = gv[...].astype(BF16)
    cp.start(gpart, grad_part).wait()


def run_self_heads(first_pair, pairs, side, lengths, projected, grad_att, logs, inner):
    n, d = grad_att.shape
    part, nk = pairs * 128, n // KEYS
    V = pltpu.VMEM
    return call(
        partial(self_heads_kernel, first_pair),
        [SMEM, SMEM, ANY, ANY, VMEM, VMEM],
        [(shape((n, 3 * part), BF16), ANY)],
        [
            V((n, part), BF16), V((n, part), BF16), V((n, part), BF16), V((n, part), BF16),
            V((pairs, nk, 2 * KEYS, 128), BF16), V((pairs, nk, 128, 2 * KEYS), BF16), V((pairs, nk, 2 * KEYS, 128), BF16),
            V((part, ROWS), F32), V((n, part), F32), V((n, part), F32), V((n, 3 * part), BF16),
            pltpu.SemaphoreType.DMA((5,)),
        ],
        5_000_000_000, 6_000_000, name="self_heads",
    )(side, lengths, projected, grad_att, logs, inner)[0]


def self_close_kernel(
    side_ref, halting, cotangent, grad_direct, grad_sum, grad_projected, weight_in,
    input_grad,
    cot, gdir, gsum, gproj, win, ingrad, sems, out_sems,
):
    side = side_ref[0]
    n, width = cot.shape
    blocks = n // ROWS
    cp = Copies(sems)
    ins = [
        cp.start(a, b)
        for a, b in (
            (grad_projected, gproj), (weight_in, win), (grad_sum, gsum), (cotangent, cot), (grad_direct, gdir),
        )
    ]
    outs = RowCopies([(ingrad, input_grad)], out_sems, blocks)
    for c in ins:
        c.wait()

    def one(i, carried):
        rows = block_rows(i)
        ingrad[rows, :] = gsum[rows, :] + mul_nt(gproj[rows, :], win[...])

        @pl.when(side == 0)
        def _():
            ingrad[rows, :] += gdir[rows, :]

        @pl.when(side == 1)
        def _():
            running = column(halting[:, block_rows(i)].astype(F32))
            ingrad[rows, :] += (1.0 - running) * cot[rows, :]

        outs.start(i)
        return carried

    lax.fori_loop(0, blocks, one, 0)
    outs.wait()


def run_self_close(side, halting, cotangent, grad_direct, grad_sum, grad_projected, weight_in):
    n, d = cotangent.shape
    V = pltpu.VMEM
    sem = pltpu.SemaphoreType.DMA
    return call(
        self_close_kernel,
        [SMEM, VMEM, ANY, ANY, ANY, ANY, ANY],
        [(shape((n, d), F32), ANY)],
        [
            V((n, d), F32), V((n, d), F32), V((n, d), F32), V((n, 3 * d), BF16), V((d, 3 * d), BF16), V((n, d), F32),
            sem((5,)), sem((1, n // ROWS)),
        ],
        2_000_000_000, 12_000_000, name="self_close",
    )(side, halting, cotangent, grad_direct, grad_sum, grad_projected, weight_in)[0]


def mul_tn(left, right):
    return lax.dot_general(left, right, (((0,), (0,)), ((), ())), preferred_element_type=F32)


def half_of(value, index, axis=0):
    size = value.shape[axis] // 2
    return lax.dynamic_slice_in_dim(value, index * size, size, axis)


def exchange(value, bit):
    return lax.ppermute(value, "dp", [(i, i ^ bit) for i in range(lax.axis_size("dp"))])


def own_of(bit):
    return (lax.axis_index("dp") // bit) % 2


def joined(value, came, bit):
    own = own_of(bit)
    return jnp.concatenate([jnp.where(own == 0, value, came), jnp.where(own == 0, came, value)], axis=0)


class Flow:
    def __init__(self, value, swapped):
        bits = [1 << b for b in range(1, lax.axis_size("dp").bit_length() - 1)]
        if swapped and len(bits) > 1:
            bits[0], bits[1] = bits[1], bits[0]
        self.value = value
        self.steps = [(b, True) for b in bits] + [(b, False) for b in reversed(bits)] + [(1, False)]

    @property
    def left(self):
        return len(self.steps)

    def operand(self):
        bit, halves = self.steps[0]
        return half_of(self.value, 1 - own_of(bit)) if halves else self.value

    def land(self, came):
        bit, halves = self.steps.pop(0)
        if halves:
            kept = half_of(self.value, own_of(bit))
            self.value = (kept.astype(F32) + came.astype(F32)).astype(BF16)
        else:
            self.value = joined(self.value, came, bit)


def fold(values):
    own = own_of(1)
    came = [exchange(half_of(v, 1 - own), 1) for v in values]
    return [
        (half_of(v, own).astype(F32) + c.astype(F32)).astype(BF16) for v, c in zip(values, came)
    ]


def stage(flows, work=None, *inputs):
    flows = [f for f in flows if f.left]
    sent, values, inputs = lax.optimization_barrier(
        ([f.operand() for f in flows], [f.value for f in flows], inputs)
    )
    came = [exchange(s, f.steps[0][0]) for s, f in zip(sent, flows)]
    out = None
    if work is not None:
        out = work(*inputs)
        came, values, out = lax.optimization_barrier((came, values, out))
    for flow, value, piece in zip(flows, values, came):
        flow.value = value
        flow.land(piece)
    return out


def body(
    tokens, cotangent, lengths, halting, attention_in, attention_out, cross_first, cross_second,
    expand_weight, expand_bias, contract_weight, contract_bias, norm_gain, norm_bias,
):
    side_index = lax.axis_index("half")
    side = side_index.astype(jnp.int32).reshape((1,))
    tok, cot = tokens[0, 0], cotangent[0, 0]
    lens = lengths[:, 0]
    halt = halting[0]
    w_in, w_out, w_one, w_two = attention_in[0], attention_out[0], cross_first[0], cross_second[0]
    w1, w2 = expand_weight[0], contract_weight[0]
    gains, shifts = norm_gain[0], norm_bias[0]
    n, d = tok.shape
    ff = w1.shape[1]
    there, back = [(0, 1)], [(1, 0)]
    source_pair = lax.ppermute(jnp.concatenate([w_one, w_two], axis=0), "half", there)
    start_low, projected, attended, logs, first_sum, memory, memory_low = run_first(
        side, lens, tok, halt, w_in, w_out, w1, expand_bias, w2, contract_bias, w_one, w_two, gains, shifts
    )
    memory_in = lax.ppermute(memory_low, "half", there)
    (
        result, hidden, branch, grad_before, ffn_in, grad_first, grad_memory,
        pairs_low, crossed, grad_cross, first_low, grad_query, kept, small,
    ) = run_middle(
        side, lens, tok, halt, cot, first_sum, memory_in, source_pair[:d], source_pair[d:], w_one, w_two,
        w1, expand_bias, w2, contract_bias, gains, shifts, memory,
    )
    grad_in = lax.ppermute(grad_memory, "half", back)
    grad_in, memory_there, pairs_there = lax.optimization_barrier((grad_in, memory_in, pairs_low))
    for_source = jnp.concatenate(
        [mul_tn(memory_there, pairs_there[:, :d]), mul_tn(memory_there, pairs_there[:, d:])], axis=0
    ).astype(BF16)
    branch, grad_before, small, grad_direct, gsum, gmix, gatt, inner = run_back(
        side, halt, cot, first_sum, grad_in, kept, attended, w1, w2, w_out, gains, shifts,
        branch, grad_before, grad_first, small,
    )
    from_target = lax.ppermute(for_source, "half", back)
    contract, expand = fold(
        [mul_tn(hidden, branch).astype(BF16), mul_tn(ffn_in, grad_before).astype(BF16)]
    )
    contract, expand = Flow(contract, False), Flow(expand, True)

    def heads(g, rows_inner):
        return run_self_heads(0, d // 128, side, lens, projected, g, logs, rows_inner)

    grad_projected = stage([contract, expand], heads, gatt, inner)

    def products(gproj, mix, theirs, one, two, three, four):
        ours = jnp.concatenate([mul_tn(one, two), mul_tn(three, four)], axis=0).astype(BF16)
        low_small = small.astype(BF16)
        rest = jnp.concatenate(
            [
                mul_tn(attended, mix).astype(BF16),
                jnp.where(side_index == 0, theirs, ours),
                low_small,
                jnp.zeros((16 * lax.axis_size("dp") - low_small.shape[0], d), BF16),
            ],
            axis=0,
        )
        return fold([rest, mul_tn(start_low, gproj).astype(BF16)])

    rest, weights_in = stage(
        [contract, expand], products, grad_projected, gmix, from_target, first_low, grad_query, crossed, grad_cross
    )
    rest, weights_in = Flow(rest, False), Flow(weights_in, True)

    def close(gproj):
        return run_self_close(side, halt, cot, grad_direct, gsum, gproj, w_in)

    input_grad = stage([contract, expand, rest, weights_in], close, grad_projected)
    flows = [contract, expand, rest, weights_in]
    while contract.left:
        stage(flows)

    def widen(one, two):
        return one.astype(F32), two.astype(F32)

    contract_out, expand_out = stage(flows, widen, contract.value, expand.value)
    while rest.left:
        stage(flows)
    rest = rest.value
    small = rest[3 * d : 3 * d + SMALL_ROWS].astype(F32)
    return (
        result[None, None],
        input_grad[None, None],
        weights_in.value.astype(F32)[None],
        rest[:d].astype(F32)[None],
        rest[d : 2 * d].astype(F32)[None],
        rest[2 * d : 3 * d].astype(F32)[None],
        expand_out[None],
        small[8 : 8 + ff // d].reshape(1, ff),
        contract_out[None],
        small[6:7],
        small[0:3][None],
        small[3:6][None],
    )


def solution(mesh):
    placed = (
        P("half", "dp", None, None),
        P("half", "dp", None, None),
        P(None, "dp", None),
        P("half", "dp", None),
        P("half", None, None),
        P("half", None, None),
        P("half", None, None),
        P("half", None, None),
        P("half", None, None),
        P("half", None),
        P("half", None, None),
        P("half", None),
        P("half", None, None),
        P("half", None, None),
    )
    return jax.shard_map(
        body,
        mesh=mesh,
        in_specs=placed,
        out_specs=(
            P("half", "dp", None, None),
            P("half", "dp", None, None),
            P("half", None, None),
            P("half", None, None),
            P("half", None, None),
            P("half", None, None),
            P("half", None, None),
            P("half", None),
            P("half", None, None),
            P("half", None),
            P("half", None, None),
            P("half", None, None),
        ),
        check_vma=False,
    )
```

```python
from functools import partial
import math

import jax
import jax.numpy as jnp
from jax import lax
from jax.experimental import pallas as pl
from jax.experimental.pallas import tpu as pltpu
from jax.sharding import PartitionSpec as P

HEADS = 8
STEP = 2
EPSILON = 1e-06
LONGEST = 256
ROWS = 256
KEYS = 128
PIECE = 512
MASKED = -1e30
VMEM_BYTES = 48 * 1024 * 1024
FIRST_BYTES = 46 * 1024 * 1024
SECOND_BYTES = 46 * 1024 * 1024
MIDDLE_BYTES = 60 * 1024 * 1024
BACK_BYTES = 42 * 1024 * 1024
BIG = 512
F32 = jnp.float32
BF16 = jnp.bfloat16


def mul(left, right):
    return jnp.dot(left, right, preferred_element_type=F32)


def mul_nt(left, right):
    return lax.dot_general(left, right, (((1,), (1,)), ((), ())), preferred_element_type=F32)


def iota(shape, axis):
    return lax.broadcasted_iota(jnp.int32, shape, axis)


def norm_parts(summed):
    center = summed - jnp.mean(summed, axis=-1, keepdims=True)
    rate = lax.rsqrt(jnp.mean(center * center, axis=-1, keepdims=True) + EPSILON)
    return center * rate, rate


def norm_back(grad, unit, rate, gain):
    scaled = grad * gain
    return rate * (
        scaled
        - jnp.mean(scaled, axis=-1, keepdims=True)
        - unit * jnp.mean(scaled * unit, axis=-1, keepdims=True)
    )


GATE_ONE = math.sqrt(2.0 / math.pi)
GATE_THREE = GATE_ONE * 0.044715


def gate(before):
    bent = jnp.tanh(before * (GATE_ONE + GATE_THREE * (before * before)))
    return before * (0.5 + 0.5 * bent)


def gate_and_slope(before):
    square = before * before
    share = 0.5 + 0.5 * jnp.tanh(before * (GATE_ONE + GATE_THREE * square))
    gated = before * share
    return gated, share + gated * ((1.0 - share) * (2 * GATE_ONE + 6 * GATE_THREE * square))


def bounds(lengths, side, key_side, block, causal):
    first_row = block * ROWS
    last_row = first_row + ROWS - 1
    place = first_row + iota((1, ROWS), 1)
    low = jnp.zeros((1, ROWS), jnp.int32)
    high = jnp.zeros((1, ROWS), jnp.int32)
    least = jnp.int32(0)
    most = jnp.int32(0)
    at = jnp.int32(0)
    key_at = jnp.int32(0)
    for k in range(lengths.shape[1]):
        end = at + lengths[side, k]
        key_end = key_at + lengths[key_side, k]
        inside = (place >= at) & (place < end)
        low = jnp.where(inside, key_at, low)
        high = jnp.where(inside, key_end, high)
        least = jnp.where((first_row >= at) & (first_row < end), key_at, least)
        most = jnp.where((last_row >= at) & (last_row < end), key_end, most)
        at, key_at = end, key_end
    if causal is not None:
        high = jnp.where(causal, jnp.minimum(high, place + 1), high)
        most = jnp.where(causal, jnp.minimum(most, last_row + 1), most)
    return low, high, least // KEYS, (most + KEYS - 1) // KEYS


def keep_pair(block, axis):
    place = iota(block.shape, axis)
    half = block.shape[axis] // 2
    zero = jnp.zeros_like(block)
    return jnp.concatenate(
        [jnp.where(place < half, block, zero), jnp.where(place >= half, block, zero)],
        axis=1 - axis,
    )


def split_heads(source, stacked, pairs):
    block, base = source
    for p in range(pairs):
        for t in range(block.shape[0] // KEYS):
            part = block[t * KEYS : (t + 1) * KEYS, p * 128 : (p + 1) * 128]
            stacked[p, base + t] = keep_pair(part, 1)


def split_heads_turned(source, stacked, pairs):
    block, base = source
    turned = block.T
    for p in range(pairs):
        for t in range(block.shape[0] // KEYS):
            part = turned[p * 128 : (p + 1) * 128, t * KEYS : (t + 1) * KEYS]
            stacked[p, base + t] = keep_pair(part, 0)


def mask_bias(block_index, low, high):
    key_place = block_index * KEYS + iota((KEYS, ROWS), 0)
    return jnp.where((key_place >= low) & (key_place < high), 0.0, MASKED)


def attend_block(queries, keys, values_turned, span, mixed, top, total):
    low, high, least, most = span
    pairs = keys.shape[0]
    mixed[...] = jnp.zeros_like(mixed)
    top[...] = jnp.full(top.shape, MASKED, F32)
    total[...] = jnp.zeros_like(total)

    def one(j, carried):
        bias = mask_bias(j, low, high)
        old = top[...]
        scores = [mul_nt(keys[p, j], queries[:, p * 128 : (p + 1) * 128]) for p in range(pairs)]
        parts = [scores[h // 2][(h % 2) * KEYS : (h % 2 + 1) * KEYS] + bias for h in range(2 * pairs)]
        new = jnp.maximum(old, jnp.concatenate([jnp.max(t, axis=0, keepdims=True) for t in parts], axis=0))
        fade = jnp.exp(old - new)
        weights = [jnp.exp(t - new[h : h + 1]) for h, t in enumerate(parts)]
        total[...] = total[...] * fade + jnp.concatenate(
            [jnp.sum(w, axis=0, keepdims=True) for w in weights], axis=0
        )
        top[...] = new
        for p in range(pairs):
            pair = jnp.concatenate([weights[2 * p].astype(BF16), weights[2 * p + 1].astype(BF16)], axis=0)
            added = mul(values_turned[p, j], pair)
            for u in range(2):
                at = p * 128 + u * 64
                mixed[at : at + 64, :] = (
                    mixed[at : at + 64, :] * fade[2 * p + u : 2 * p + u + 1] + added[u * 64 : (u + 1) * 64]
                )
        return carried

    lax.fori_loop(least, most, one, 0)
    for h in range(2 * pairs):
        rate = 1.0 / total[h : h + 1, :]
        mixed[h * 64 : (h + 1) * 64, :] = mixed[h * 64 : (h + 1) * 64, :] * rate
    top[...] = top[...] + jnp.log(total[...])


def attend_block_back(
    queries, grads, keys, keys_turned, values, span, logs, inner, grad_queries, grad_keys, grad_values
):
    low, high, least, most = span
    pairs = keys.shape[0]
    grad_queries[...] = jnp.zeros_like(grad_queries)
    first_half = iota((KEYS, 128), 1) < 64

    def one(j, carried):
        bias = mask_bias(j, low, high)
        rows = pl.ds(pl.multiple_of(j * KEYS, KEYS), KEYS)
        lanes = [slice(p * 128, (p + 1) * 128) for p in range(pairs)]
        scores = [mul_nt(keys[p, j], queries[:, lanes[p]]) for p in range(pairs)]
        grad_probs = [mul_nt(values[p, j], grads[:, lanes[p]]) for p in range(pairs)]
        probs, grad_scores = [], []
        for h in range(2 * pairs):
            part = slice((h % 2) * KEYS, (h % 2 + 1) * KEYS)
            prob = jnp.exp(scores[h // 2][part] + bias - logs[h : h + 1, :])
            probs.append(prob.astype(BF16))
            grad_scores.append((prob * (grad_probs[h // 2][part] - inner[h : h + 1, :])).astype(BF16))
        for p in range(pairs):
            both = mul(jnp.concatenate(probs[2 * p : 2 * p + 2], axis=0), grads[:, lanes[p]])
            grad_values[rows, lanes[p]] += jnp.where(first_half, both[:KEYS], both[KEYS:])
        for p in range(pairs):
            grad_pair = jnp.concatenate(grad_scores[2 * p : 2 * p + 2], axis=0)
            both = mul(grad_pair, queries[:, lanes[p]])
            grad_keys[rows, lanes[p]] += jnp.where(first_half, both[:KEYS], both[KEYS:])
            grad_queries[lanes[p], :] += mul(keys_turned[p, j], grad_pair)
        return carried

    lax.fori_loop(least, most, one, 0)


def row_inner(grads, mixed):
    width = grads.shape[1]
    head_of = iota((16, width), 1) // (width // HEADS)
    picks = (head_of == iota((16, width), 0)).astype(BF16)
    product = grads.astype(F32) * mixed.astype(F32)
    big = product.astype(BF16)
    small = (product - big.astype(F32)).astype(BF16)
    return mul_nt(picks, big) + mul_nt(picks, small)


def column(row):
    return jnp.broadcast_to(row, (128, row.shape[1])).T[:, :1]


class Copies:
    def __init__(self, sems):
        self.sems = sems
        self.used = 0

    def start(self, source, target):
        copy = pltpu.make_async_copy(source, target, self.sems.at[self.used])
        self.used += 1
        copy.start()
        return copy


def block_rows(i):
    return pl.ds(pl.multiple_of(i * ROWS, ROWS), ROWS)


def big_rows(i):
    return pl.ds(pl.multiple_of(i * BIG, BIG), BIG)


class RowCopies:
    def __init__(self, pairs, sems, blocks):
        self.pairs, self.sems, self.blocks = pairs, sems, blocks

    def copy(self, k, i):
        source, target = self.pairs[k]
        rows = big_rows(i)
        return pltpu.make_async_copy(source.at[rows, :], target.at[rows, :], self.sems.at[k, i])

    def start(self, i, first=None):
        for k in range(first or len(self.pairs)):
            self.copy(k, i).start()

    def wait(self):
        for i in range(self.blocks):
            for k in range(len(self.pairs)):
                self.copy(k, i).wait()


def colsum(values):
    return jnp.sum(values, axis=0, keepdims=True)


def ffn_forward(low_in, base, weights):
    expand_w, expand_b, contract_w, contract_b = weights
    total = base + contract_b[...]
    for c in range(expand_w.shape[1] // PIECE):
        part = slice(c * PIECE, (c + 1) * PIECE)
        before = mul(low_in, expand_w[:, part]) + expand_b[:, part]
        total = total + mul(gate(before).astype(BF16), contract_w[part, :])
    return total


def ffn_forward_kept(low_in, base, weights, hidden, slopes):
    expand_w, expand_b, contract_w, contract_b = weights
    total = base + contract_b[...]
    for c in range(expand_w.shape[1] // PIECE):
        part = slice(c * PIECE, (c + 1) * PIECE)
        before = mul(low_in, expand_w[:, part]) + expand_b[:, part]
        gated, slope = gate_and_slope(before)
        gated = gated.astype(BF16)
        hidden(part, gated)
        slopes[:, part] = slope.astype(BF16)
        total = total + mul(gated, contract_w[part, :])
    return total


def ffn_back(grad_summed, weights, slopes, grad_before, small):
    expand_w, _, contract_w, _ = weights
    branch = grad_summed.astype(BF16)
    grad_in = grad_summed
    for c in range(expand_w.shape[1] // PIECE):
        part = slice(c * PIECE, (c + 1) * PIECE)
        pushed = (mul_nt(branch, contract_w[part, :]) * slopes[:, part].astype(F32)).astype(BF16)
        grad_before(part, pushed)
        small[8 + c : 9 + c, :] += colsum(pushed.astype(F32))
        grad_in = grad_in + mul_nt(pushed, expand_w[:, part])
    return branch, grad_in


def first_rows(
    side, lengths, halting, big, tok, proj, keys, values_turned, start, wout, weights, gains, shifts,
    mixed, top, total, logs, att, fsum, mem, meml, width, ready,
):
    scale = BF16(1.0 / math.sqrt(width // HEADS))

    def attend(t, carried):
        rows = block_rows(t)
        i = big * (BIG // ROWS) + t
        attend_block(
            proj[rows, :width] * scale, keys, values_turned, bounds(lengths, side, side, i, side == 1), mixed, top, total
        )
        logs[t] = top[...]
        att[rows, :] = mixed[...].astype(BF16).T
        return carried

    lax.fori_loop(0, BIG // ROWS, attend, 0)
    ready()
    summed = start[...] + mul(att[...], wout[...])
    fsum[...] = summed

    @pl.when(side == 0)
    def _():
        first = norm_parts(summed)[0] * gains[0:1, :] + shifts[0:1, :]
        tail = norm_parts(ffn_forward(first.astype(BF16), first, weights))[0] * gains[1:2, :] + shifts[1:2, :]
        state = tok[...].astype(F32)
        running = column(halting[:, big * BIG : (big + 1) * BIG].astype(F32))
        kept = norm_parts(state + running * (tail - state))[0] * gains[2:3, :] + shifts[2:3, :]
        mem[...] = kept
        meml[...] = kept.astype(BF16)


def first_kernel(
    side_ref, lengths, tokens, halting, weight_in, weight_out, expand_w, expand_b, contract_w, contract_b, gains, shifts,
    start_low, projected, attended, logs, first_sum, memory, memory_low, keys_out,
    w1, w2, wout, start, proj, keys, values_turned,
    tok, win, table_big, table_small, mixed, top, total,
    att, fsum, mem, meml, slow, sems, early_sems,
):
    side = side_ref[0]
    blocks = tokens.shape[0] // BIG
    width = tokens.shape[1]
    pairs = width // 128
    cp = Copies(sems)
    c_tok = cp.start(tokens, tok)
    c_in = cp.start(weight_in, win)
    c_out = cp.start(weight_out, wout)
    c_w1 = cp.start(expand_w, w1)
    c_w2 = cp.start(contract_w, w2)
    early = RowCopies([(slow, start_low), (proj, projected)], early_sems, blocks)

    half = width // 2
    rate = jnp.exp(iota((16, half), 1).astype(F32) * (-math.log(10000.0) / half))
    fine = iota((16, half), 0).astype(F32) * rate
    coarse = fine * 16.0
    fine_s, fine_c, coarse_s, coarse_c = jnp.sin(fine), jnp.cos(fine), jnp.sin(coarse), jnp.cos(coarse)
    step_s, step_c = fine_s[STEP : STEP + 1], fine_c[STEP : STEP + 1]
    for a in range(LONGEST // 16):
        s, c = coarse_s[a : a + 1], coarse_c[a : a + 1]
        whole = jnp.concatenate(
            [s * fine_c + c * fine_s + step_s, c * fine_c - s * fine_s + step_c], axis=1
        )
        big = whole.astype(BF16)
        table_big[a * 16 : (a + 1) * 16, :] = big
        table_small[a * 16 : (a + 1) * 16, :] = (whole - big.astype(F32)).astype(BF16)

    lane = iota((1, 128), 1)
    begins = jnp.zeros((1, 128), jnp.int32)
    at = jnp.int32(0)
    for k in range(lengths.shape[1]):
        begins = jnp.where(lane == k, at, begins)
        at = at + lengths[side, k]
    c_tok.wait()
    c_in.wait()

    def prepare(i, carried):
        rows = big_rows(i)
        place = i * BIG + iota((BIG, 1), 0)
        began = jnp.max(jnp.where(place >= begins, begins, 0), axis=1, keepdims=True)
        picks = (iota((BIG, LONGEST), 1) == place - began).astype(F32).astype(BF16)
        block = tok[rows, :].astype(F32) + (mul(picks, table_big[...]) + mul(picks, table_small[...]))
        start[rows, :] = block
        low = block.astype(BF16)
        slow[rows, :] = low
        sent = mul(low, win[...]).astype(BF16)
        proj[rows, :] = sent
        split_heads((sent[:, width : 2 * width], (BIG // KEYS) * i), keys, pairs)
        split_heads_turned((sent[:, 2 * width :], (BIG // KEYS) * i), values_turned, pairs)
        early.start(i)
        return carried

    lax.fori_loop(0, blocks, prepare, 0)
    c_keys = cp.start(keys, keys_out)

    def ready():
        for c in (c_out, c_w1, c_w2):
            c.wait()

    rows = pl.ds(0, BIG)
    first_rows(
        side, lengths, halting, 0, tok.at[rows, :], proj.at[rows, :], keys, values_turned, start.at[rows, :], wout,
        (w1, expand_b, w2, contract_b), gains, shifts, mixed, top, total, logs, att, fsum, mem, meml, width, ready,
    )
    outs = [
        cp.start(att, attended.at[rows, :]), cp.start(fsum, first_sum.at[rows, :]),
    ]

    @pl.when(side == 0)
    def _():
        a = cp.start(mem, memory.at[rows, :])
        b = cp.start(meml, memory_low)
        a.wait()
        b.wait()

    early.wait()
    for c in outs + [c_keys]:
        c.wait()


def second_kernel(
    side_ref, lengths, tokens, halting, wout, w1, expand_b, w2, contract_b, gains, shifts,
    proj, keys, values_turned, start, attended_in, first_sum_in, memory_in,
    attended, logs, first_sum, memory, memory_low,
    tok, mixed, top, total, att, fsum, mem, meml, sems,
):
    side = side_ref[0]
    width = tok.shape[1]
    rows = pl.ds(BIG, BIG)
    cp = Copies(sems)
    c_tok = cp.start(tokens.at[rows, :], tok)
    first_rows(
        side, lengths, halting, 1, tok, proj.at[rows, :], keys, values_turned, start.at[rows, :], wout,
        (w1, expand_b, w2, contract_b), gains, shifts, mixed, top, total, logs, att, fsum, mem, meml, width, c_tok.wait,
    )
    outs = [
        cp.start(att, attended.at[rows, :]), cp.start(fsum, first_sum.at[rows, :]),
    ]

    @pl.when(side == 0)
    def _():
        a = cp.start(mem, memory.at[rows, :])
        b = cp.start(meml, memory_low)
        a.wait()
        b.wait()

    for c in outs:
        c.wait()


ANY = pl.BlockSpec(memory_space=pl.ANY)
SMEM = pl.BlockSpec(memory_space=pltpu.SMEM)
VMEM = pl.BlockSpec(memory_space=pltpu.VMEM)
HELD = pl.BlockSpec(memory_space=pltpu.VMEM)


def shape(s, d):
    return jax.ShapeDtypeStruct(s, d)


def held(s, d):
    return (shape(s, d), HELD)


def call(kernel, ins, outs, scratch, flops, moved, aliases=None, name=None, vmem=VMEM_BYTES):
    made = pl.pallas_call(
        kernel,
        in_specs=ins,
        out_specs=[spec for _, spec in outs],
        out_shape=[
            pltpu.HBM(o.shape, o.dtype) if spec is ANY else pltpu.VMEM(o.shape, o.dtype) if spec is HELD else o
            for o, spec in outs
        ],
        scratch_shapes=scratch,
        input_output_aliases=aliases or {},
        compiler_params=pltpu.CompilerParams(vmem_limit_bytes=vmem),
        cost_estimate=pl.CostEstimate(flops=flops, bytes_accessed=moved, transcendentals=0),
        name=name,
    )

    def run(*operands):
        places = [pltpu.HBM if spec is ANY else pltpu.VMEM if spec is HELD else None for spec in ins]
        return made(
            *(
                o if place is None else pltpu.with_memory_space_constraint(o, place)
                for o, place in zip(operands, places)
            )
        )

    return run


def run_first(side, lengths, tokens, halting, weight_in, weight_out, expand_w, expand_b, contract_w, contract_b, gains, shifts):
    n, d = tokens.shape
    ff = expand_w.shape[1]
    pairs, nk = d // 128, n // KEYS
    V = pltpu.VMEM
    sem = pltpu.SemaphoreType.DMA
    return call(
        first_kernel,
        [SMEM, SMEM, ANY, VMEM, ANY, ANY, ANY, VMEM, ANY, VMEM, VMEM, VMEM],
        [
            (shape((n, d), BF16), ANY),
            (shape((n, 3 * d), BF16), ANY),
            (shape((n, d), BF16), ANY),
            (shape((BIG // ROWS, HEADS, ROWS), F32), VMEM),
            (shape((n, d), F32), ANY),
            (shape((n, d), F32), ANY),
            (shape((BIG, d), BF16), ANY),
            (shape((pairs, nk, 2 * KEYS, 128), BF16), ANY),
            held((d, ff), BF16), held((ff, d), BF16), held((d, d), BF16),
            held((n, d), F32),
            held((n, 3 * d), BF16),
            held((pairs, nk, 2 * KEYS, 128), BF16),
            held((pairs, nk, 128, 2 * KEYS), BF16),
        ],
        [
            V((n, d), BF16), V((d, 3 * d), BF16),
            V((LONGEST, d), BF16), V((LONGEST, d), BF16),
            V((d, ROWS), F32), V((HEADS, ROWS), F32), V((HEADS, ROWS), F32),
            V((BIG, d), BF16), V((BIG, d), F32), V((BIG, d), F32), V((BIG, d), BF16), V((n, d), BF16),
            sem((10,)), sem((2, n // BIG)),
        ],
        8_000_000_000, 20_000_000, name="first_half", vmem=FIRST_BYTES,
    )(side, lengths, tokens, halting, weight_in, weight_out, expand_w, expand_b, contract_w, contract_b, gains, shifts)


def run_second(side, lengths, tokens, halting, weight_out, expand_w, expand_b, contract_w, contract_b, gains, shifts, projected, keys, turned, start, attended, first_sum, memory):
    n, d = tokens.shape
    ff = expand_w.shape[1]
    V = pltpu.VMEM
    return call(
        second_kernel,
        [SMEM, SMEM, ANY, VMEM, HELD, HELD, VMEM, HELD, VMEM, VMEM, VMEM, HELD, HELD, HELD, HELD, ANY, ANY, ANY],
        [
            (shape((n, d), BF16), ANY),
            (shape((BIG // ROWS, HEADS, ROWS), F32), VMEM),
            (shape((n, d), F32), ANY),
            (shape((n, d), F32), ANY),
            (shape((BIG, d), BF16), ANY),
        ],
        [
            V((BIG, d), BF16),
            V((d, ROWS), F32), V((HEADS, ROWS), F32), V((HEADS, ROWS), F32),
            V((BIG, d), BF16), V((BIG, d), F32), V((BIG, d), F32), V((BIG, d), BF16),
            pltpu.SemaphoreType.DMA((5,)),
        ],
        6_000_000_000, 16_000_000, aliases={15: 0, 16: 2, 17: 3}, name="second_half", vmem=SECOND_BYTES,
    )(side, lengths, tokens, halting, weight_out, expand_w, expand_b, contract_w, contract_b, gains, shifts, projected, keys, turned, start, attended, first_sum, memory)


SMALL_ROWS = 16


def middle_kernel(
    side_ref, lengths, tokens, halting, cotangent, first_sum, memory_a, memory_b, key_w, value_w, cross_w, mix_w,
    expand_w, expand_b, contract_w, contract_b, gains, shifts, memory,
    result, hidden, branch, grad_before, ffn_in, grad_first, grad_memory_a, grad_memory_b,
    pairs_low, crossed, grad_cross, first_low, grad_query, kept, small,
    mlow, kw, vw, cw, mw, w1, w2, tok, cot, fsum, keys, keys_t, values, values_t, slopes,
    mixed, top, total, logs, inner, que, gmix, gqt, gk, gv,
    res, hid, bra, gbef, fin, gfirst, gmem, plow, cro, gcro, flow, gqry, sems, out_sems, last_sems,
):
    side = side_ref[0]
    n, width = tok.shape
    blocks = n // BIG
    subs = BIG // ROWS
    pairs = width // 128
    scale = 1.0 / math.sqrt(width // HEADS)
    weights = (w1, expand_b, w2, contract_b)

    @pl.when(side == 0)
    def _():
        cp = Copies(sems)
        ins = [
            cp.start(a, b) for a, b in ((first_sum, fsum), (tokens, tok), (expand_w, w1), (contract_w, w2))
        ]
        outs = RowCopies(
            [(hid, hidden), (gbef, grad_before), (fin, ffn_in), (gfirst, grad_first), (res, kept)], out_sems, blocks
        )
        small[...] = jnp.zeros_like(small)
        for c in ins:
            c.wait()

        def one(i, carried):
            rows = big_rows(i)
            first = norm_parts(fsum[rows, :])[0] * gains[0:1, :] + shifts[0:1, :]
            low = first.astype(BF16)
            fin[rows, :] = low

            def keep_hidden(part, value):
                hid[rows, part] = value

            summed = ffn_forward_kept(low, first, weights, keep_hidden, slopes)
            gbef[rows, :] = slopes[...]
            res[rows, :] = summed
            tail = norm_parts(summed)[0] * gains[1:2, :] + shifts[1:2, :]
            state = tok[rows, :].astype(F32)
            running = column(halting[:, rows].astype(F32))
            gfirst[rows, :] = state + running * (tail - state)
            outs.start(i)
            return carried

        lax.fori_loop(0, blocks, one, 0)
        outs.wait()

    @pl.when(side == 1)
    def _():
        cp = Copies(sems)
        c_kw, c_vw = cp.start(key_w, kw), cp.start(value_w, vw)
        c_mem = [cp.start(memory_a, mlow.at[0:BIG, :]), cp.start(memory_b, mlow.at[BIG : 2 * BIG, :])]
        rest = [
            cp.start(a, b)
            for a, b in (
                (first_sum, fsum), (cross_w, cw), (mix_w, mw), (expand_w, w1), (tokens, tok), (contract_w, w2), (cotangent, cot),
            )
        ]
        outs = RowCopies(
            [
                (flow, first_low), (cro, crossed), (fin, ffn_in), (hid, hidden), (res, result),
                (bra, branch), (gbef, grad_before), (gcro, grad_cross),
            ],
            out_sems, blocks,
        )
        ends = RowCopies([(gfirst, grad_first), (gqry, grad_query), (plow, pairs_low)], last_sems, blocks)
        small[...] = jnp.zeros_like(small)
        gk[...] = jnp.zeros_like(gk)
        gv[...] = jnp.zeros_like(gv)
        for c in [c_kw, c_vw] + c_mem:
            c.wait()

        def prepare(i, carried):
            low = mlow[big_rows(i), :]
            key = mul(low, kw[...]).astype(BF16)
            value = mul(low, vw[...]).astype(BF16)
            split_heads((key, (BIG // KEYS) * i), keys, pairs)
            split_heads((value, (BIG // KEYS) * i), values, pairs)
            split_heads_turned((key, (BIG // KEYS) * i), keys_t, pairs)
            split_heads_turned((value, (BIG // KEYS) * i), values_t, pairs)
            return carried

        lax.fori_loop(0, blocks, prepare, 0)
        for c in rest[:2]:
            c.wait()

        def once(i, copies):
            @pl.when(i == 0)
            def _():
                for c in copies:
                    c.wait()

        def one(i, carried):
            rows = big_rows(i)
            first = norm_parts(fsum[rows, :])[0] * gains[0:1, :] + shifts[0:1, :]
            fsum[rows, :] = first
            low = first.astype(BF16)
            flow[rows, :] = low
            que[...] = mul(low, cw[...]).astype(BF16) * BF16(scale)

            def there(t, carried):
                sub = block_rows(t)
                span = bounds(lengths, 1, 0, i * subs + t, None)
                attend_block(que[sub, :], keys, values_t, span, mixed, top, total)
                logs[t] = top[...]
                cro[block_rows(i * subs + t), :] = mixed[...].astype(BF16).T
                return carried

            lax.fori_loop(0, subs, there, 0)
            once(i, rest[2:])
            unit2, rate2 = norm_parts(fsum[rows, :] + mul(cro[rows, :], mw[...]))
            second = unit2 * gains[2:3, :] + shifts[2:3, :]
            low = second.astype(BF16)
            fin[rows, :] = low

            def keep_hidden(part, value):
                hid[rows, part] = value

            def keep_before(part, value):
                gbef[rows, part] = value

            unit1, rate1 = norm_parts(ffn_forward_kept(low, second, weights, keep_hidden, slopes))
            state = tok[rows, :].astype(F32)
            running = column(halting[:, rows].astype(F32))
            res[rows, :] = state + running * (unit1 * gains[1:2, :] + shifts[1:2, :] - state)
            grad = running * cot[rows, :]
            small[1:2, :] += colsum(grad * unit1)
            small[4:5, :] += colsum(grad)
            grad_low, grad = ffn_back(
                norm_back(grad, unit1, rate1, gains[1:2, :]), weights, slopes, keep_before, small
            )
            bra[rows, :] = grad_low
            small[6:7, :] += colsum(grad_low.astype(F32))
            small[2:3, :] += colsum(grad * unit2)
            small[5:6, :] += colsum(grad)
            grad = norm_back(grad, unit2, rate2, gains[2:3, :])
            grad_low = grad.astype(BF16)
            gcro[rows, :] = grad_low
            gfirst[rows, :] = grad
            outs.start(i)
            back = mul_nt(grad_low, mw[...]).astype(BF16)
            gmix[...] = back
            for t in range(subs):
                inner[t] = row_inner(back[t * ROWS : (t + 1) * ROWS], cro[block_rows(i * subs + t), :])

            def here(t, carried):
                sub = block_rows(t)
                span = bounds(lengths, 1, 0, i * subs + t, None)
                attend_block_back(
                    que[sub, :], gmix[sub, :], keys, keys_t, values, span, logs[t], inner[t], gqt, gk, gv
                )
                gqry[block_rows(i * subs + t), :] = (gqt[...] * scale).astype(BF16).T
                return carried

            lax.fori_loop(0, subs, here, 0)
            gfirst[rows, :] += mul_nt(gqry[rows, :], cw[...])
            ends.start(i, 2)
            return carried

        lax.fori_loop(0, blocks, one, 0)
        sends = []
        for i, target in enumerate((grad_memory_a, grad_memory_b)):
            rows = pl.ds(i * BIG, BIG)
            key = gk[rows, :].astype(BF16)
            value = gv[rows, :].astype(BF16)
            gmem[rows, :] = (mul_nt(key, kw[...]) + mul_nt(value, vw[...])).astype(BF16)
            sends.append(cp.start(gmem.at[rows, :], target))
            plow[rows, :width] = key
            plow[rows, width:] = value
            ends.copy(2, i).start()
        outs.wait()
        ends.wait()
        for c in sends:
            c.wait()


def run_middle(side, lengths, tokens, halting, cotangent, first_sum, memory_a, memory_b, key_w, value_w, cross_w, mix_w, expand_w, expand_b, contract_w, contract_b, gains, shifts, memory):
    n, d = tokens.shape
    ff = expand_w.shape[1]
    pairs, nk, subs = d // 128, n // KEYS, BIG // ROWS
    V = pltpu.VMEM
    sem = pltpu.SemaphoreType.DMA
    return call(
        middle_kernel,
        [SMEM, SMEM, ANY, VMEM, ANY, ANY, ANY, ANY, ANY, ANY, ANY, ANY, ANY, VMEM, ANY, VMEM, VMEM, VMEM, ANY],
        [
            (shape((n, d), F32), ANY),
            (shape((n, ff), BF16), ANY),
            (shape((n, d), BF16), ANY),
            (shape((n, ff), BF16), ANY),
            (shape((n, d), BF16), ANY),
            (shape((n, d), F32), ANY),
            (shape((BIG, d), BF16), ANY),
            (shape((BIG, d), BF16), ANY),
            (shape((n, 2 * d), BF16), ANY),
            (shape((n, d), BF16), ANY),
            (shape((n, d), BF16), ANY),
            (shape((n, d), BF16), ANY),
            (shape((n, d), BF16), ANY),
            (shape((n, d), F32), ANY),
            (shape((SMALL_ROWS, d), F32), VMEM),
        ],
        [
            V((n, d), BF16), V((d, d), BF16), V((d, d), BF16), V((d, d), BF16), V((d, d), BF16),
            V((d, ff), BF16), V((ff, d), BF16), V((n, d), BF16), V((n, d), F32), V((n, d), F32),
            V((pairs, nk, 2 * KEYS, 128), BF16), V((pairs, nk, 128, 2 * KEYS), BF16),
            V((pairs, nk, 2 * KEYS, 128), BF16), V((pairs, nk, 128, 2 * KEYS), BF16),
            V((BIG, ff), BF16), V((d, ROWS), F32), V((HEADS, ROWS), F32), V((HEADS, ROWS), F32),
            V((subs, HEADS, ROWS), F32), V((subs, 16, ROWS), F32), V((BIG, d), BF16), V((BIG, d), BF16),
            V((d, ROWS), F32), V((n, d), F32), V((n, d), F32),
            V((n, d), F32), V((n, ff), BF16), V((n, d), BF16), V((n, ff), BF16),
            V((n, d), BF16), V((n, d), F32), V((n, d), BF16), V((n, 2 * d), BF16), V((n, d), BF16),
            V((n, d), BF16), V((n, d), BF16), V((n, d), BF16),
            sem((13,)), sem((8, n // BIG)), sem((3, n // BIG)),
        ],
        24_000_000_000, 40_000_000, aliases={18: 0}, name="target_middle", vmem=MIDDLE_BYTES,
    )(side, lengths, tokens, halting, cotangent, first_sum, memory_a, memory_b, key_w, value_w, cross_w, mix_w, expand_w, expand_b, contract_w, contract_b, gains, shifts, memory)


def back_kernel(
    big, side_ref, halting, cotangent, first_sum, grad_memory, kept, attended, expand_w, contract_w, weight_out,
    gains, shifts, branch_in, before_in, first_in, small_in, *rest,
):
    rest = rest[5:] if big else rest
    lefts, rights = rest[:4], rest[4:7]
    if not big:
        rest = rest[7:]
    branch, grad_before, small, grad_direct, gsum, gmix, gatt, inner = rest[:8]
    rest = rest[8:]
    if not big:
        products, rest = rest[:3], rest[3:]
        left, right, made = rest[-3:]
    gmem, cot, fsum, att, gdir, step, sum1, w1, w2, wout, slo, bra, gbef, sems = rest[:14]
    side = side_ref[0]
    rows = pl.ds(big * BIG, BIG)
    cp = Copies(sems)
    c_first = cp.start(first_in.at[rows, :], step)
    small[...] = small_in[...]

    def start_open():
        return [
            cp.start(a, b)
            for a, b in ((first_sum.at[rows, :], fsum), (attended.at[rows, :], att), (weight_out, wout))
        ]

    def open_block(grad, copies):
        copies[0].wait()
        unit, rate = norm_parts(fsum[...])
        small[0:1, :] += colsum(grad * unit)
        small[3:4, :] += colsum(grad)
        grad = norm_back(grad, unit, rate, gains[0:1, :])
        gsum[rows, :] = grad
        grad_low = grad.astype(BF16)
        gmix[rows, :] = grad_low
        copies[1].wait()
        copies[2].wait()
        grad_mixed = mul_nt(grad_low, wout[...]).astype(BF16)
        gatt[rows, :] = grad_mixed
        for t in range(BIG // ROWS):
            part = slice(t * ROWS, (t + 1) * ROWS)
            inner[t] = row_inner(grad_mixed[part], att[part, :])

    @pl.when(side == 0)
    def _():
        c_mem = cp.start(grad_memory, gmem)
        c_cot = cp.start(cotangent.at[rows, :], cot)
        c_sum1 = cp.start(kept.at[rows, :], sum1)
        parts = [slice(c * PIECE, (c + 1) * PIECE) for c in range(w1.shape[1] // PIECE)]
        pieces = [
            [
                cp.start(contract_w.at[part, :], w2.at[part, :]),
                cp.start(before_in.at[rows, part], slo.at[:, part]),
                cp.start(expand_w.at[:, part], w1.at[:, part]),
            ]
            for part in parts
        ]
        opening = start_open()
        running = column(halting[:, big * BIG : (big + 1) * BIG].astype(F32))
        c_first.wait()
        unit2, rate2 = norm_parts(step[...])
        c_mem.wait()
        c_cot.wait()
        grad = cot[...] + gmem[...].astype(F32)
        small[2:3, :] += colsum(grad * unit2)
        small[5:6, :] += colsum(grad)
        grad = norm_back(grad, unit2, rate2, gains[2:3, :])
        gdir[...] = (1.0 - running) * grad
        outs = [cp.start(gdir, grad_direct.at[rows, :])]
        grad = running * grad
        c_sum1.wait()
        unit1, rate1 = norm_parts(sum1[...])
        small[1:2, :] += colsum(grad * unit1)
        small[4:5, :] += colsum(grad)
        grad_summed = norm_back(grad, unit1, rate1, gains[1:2, :])
        low = grad_summed.astype(BF16)
        bra[...] = low
        outs.append(cp.start(bra, branch.at[rows, :]))
        small[6:7, :] += colsum(low.astype(F32))
        grad_in = grad_summed
        for c, part in enumerate(parts):
            for copy in pieces[c]:
                copy.wait()
            pushed = (mul_nt(low, w2[part, :]) * slo[:, part].astype(F32)).astype(BF16)
            gbef[:, part] = pushed
            outs.append(cp.start(gbef.at[:, part], grad_before.at[rows, part]))
            small[8 + c : 9 + c, :] += colsum(pushed.astype(F32))
            grad_in = grad_in + mul_nt(pushed, w1[:, part])
        open_block(grad_in, opening)
        for c in outs:
            c.wait()

    @pl.when(side == 1)
    def _():
        opening = start_open()
        if not big:
            n, width = left.shape[1:]
            ours_one, ours_two, for_source = products
            ins = []
            for k, (a, b) in enumerate(zip(lefts[:2], rights[:2])):
                ins.append([cp.start(a, left.at[k]), cp.start(b, right.at[k])])
            lefts_there = [
                cp.start(a, left.at[2, t * BIG : (t + 1) * BIG, :]) for t, a in enumerate(lefts[2:])
            ]
            ins.append(lefts_there + [cp.start(rights[2].at[:, 0:width], right.at[2])])
            ins.append([cp.start(rights[2].at[:, width : 2 * width], right.at[3])])
            outs = []
            for k in range(4):
                for c in ins[k]:
                    c.wait()
                made[k] = mul(left[min(k, 2)].T, right[k]).astype(BF16)
                target = (ours_one, ours_two, for_source.at[0:width, :], for_source.at[width : 2 * width, :])[k]
                outs.append(cp.start(made.at[k], target))
        c_first.wait()
        open_block(step[...], opening)
        if not big:
            for c in outs:
                c.wait()


def run_back(big, side, halting, cotangent, first_sum, grad_memory, kept, attended, expand_w, contract_w, weight_out, gains, shifts, branch, before, first, small, earlier):
    n, d = first_sum.shape
    ff = expand_w.shape[1]
    V = pltpu.VMEM
    aliases = {12: 0, 13: 1, 15: 2}
    ins = [SMEM, VMEM] + [ANY] * 8 + [VMEM, VMEM, ANY, ANY, ANY, VMEM]
    outs = [
        (shape((n, d), BF16), ANY), (shape((n, ff), BF16), ANY), (shape((SMALL_ROWS, d), F32), VMEM),
        (shape((n, d), F32), ANY), held((n, d), F32), held((n, d), BF16), held((n, d), BF16),
        (shape((BIG // ROWS, 16, ROWS), F32), VMEM),
    ]
    scratch = [
        V((BIG, d), BF16), V((BIG, d), F32), V((BIG, d), F32), V((BIG, d), BF16), V((BIG, d), F32),
        V((BIG, d), F32), V((BIG, d), F32), V((d, ff), BF16), V((ff, d), BF16), V((d, d), BF16),
        V((BIG, ff), BF16), V((BIG, d), BF16), V((BIG, ff), BF16),
        pltpu.SemaphoreType.DMA((44,)),
    ]
    if big:
        aliases.update({16: 3, 17: 4, 18: 5, 19: 6})
        ins += [ANY, HELD, HELD, HELD, VMEM]
    else:
        ins += [ANY] * 7
        outs += [(shape((d, d), BF16), ANY), (shape((d, d), BF16), ANY), (shape((2 * d, d), BF16), ANY)]
        scratch += [V((3, n, d), BF16), V((4, n, d), BF16), V((4, d, d), BF16)]
    return call(
        partial(back_kernel, big),
        ins,
        outs,
        scratch,
        4_000_000_000, 16_000_000, aliases=aliases, name="norms_back", vmem=BACK_BYTES,
    )(side, halting, cotangent, first_sum, grad_memory, kept, attended, expand_w, contract_w, weight_out, gains, shifts, branch, before, first, small, *earlier)


def self_heads_kernel(
    first_pair, side_ref, lengths, projected, grad_att, logs_a, logs_b, inner_a, inner_b, keys_in,
    gpart,
    que, key, val, keys, keys_t, values, gqt, gk, gv, sems,
):
    side = side_ref[0]
    n, part = que.shape
    width = grad_att.shape[1]
    blocks = n // ROWS
    pairs = part // 128
    scale = 1.0 / math.sqrt(width // HEADS)
    cp = Copies(sems)
    at = first_pair * 128
    c_key = cp.start(projected.at[:, width + at : width + at + part], key)
    c_val = cp.start(projected.at[:, 2 * width + at : 2 * width + at + part], val)
    c_keys = cp.start(keys_in, keys)
    c_que = cp.start(projected.at[:, at : at + part], que)
    gk[...] = jnp.zeros_like(gk)
    gv[...] = jnp.zeros_like(gv)
    c_key.wait()
    c_val.wait()

    def prepare(i, carried):
        rows = block_rows(i)
        split_heads_turned((key[rows, :], 2 * i), keys_t, pairs)
        split_heads((val[rows, :], 2 * i), values, pairs)
        return carried

    lax.fori_loop(0, blocks, prepare, 0)
    c_que.wait()
    c_keys.wait()

    for half, (logs, inner) in enumerate(((logs_a, inner_a), (logs_b, inner_b))):

        def one(t, carried):
            i = half * (BIG // ROWS) + t
            rows = block_rows(i)
            queries = que[rows, :] * BF16(scale)
            span = bounds(lengths, side, side, i, side == 1)
            attend_block_back(
                queries, grad_att[rows, at : at + part], keys, keys_t, values, span, logs[t], inner[t], gqt, gk, gv
            )
            gpart[rows, :part] = (gqt[...] * scale).astype(BF16).T
            return carried

        lax.fori_loop(0, BIG // ROWS, one, 0)
    gpart[:, part : 2 * part] = gk[...].astype(BF16)
    gpart[:, 2 * part :] = gv[...].astype(BF16)


def run_self_heads(first_pair, pairs, side, lengths, projected, grad_att, logs, inner, keys):
    n, d = grad_att.shape
    part, nk = pairs * 128, n // KEYS
    V = pltpu.VMEM
    return call(
        partial(self_heads_kernel, first_pair),
        [SMEM, SMEM, ANY, HELD, VMEM, VMEM, VMEM, VMEM, ANY],
        [held((n, 3 * part), BF16)],
        [
            V((n, part), BF16), V((n, part), BF16), V((n, part), BF16),
            V((pairs, nk, 2 * KEYS, 128), BF16), V((pairs, nk, 128, 2 * KEYS), BF16), V((pairs, nk, 2 * KEYS, 128), BF16),
            V((part, ROWS), F32), V((n, part), F32), V((n, part), F32),
            pltpu.SemaphoreType.DMA((5,)),
        ],
        5_000_000_000, 6_000_000, name="self_heads",
    )(side, lengths, projected, grad_att, *logs, *inner, keys)[0]


def self_close_kernel(
    side_ref, halting, cotangent, grad_direct, gsum, gproj, weight_in,
    input_grad,
    cot, gdir, win, ingrad, sems, out_sems,
):
    side = side_ref[0]
    n, width = cot.shape
    blocks = n // BIG
    cp = Copies(sems)
    ins = [
        cp.start(a, b)
        for a, b in (
            (weight_in, win), (cotangent, cot), (grad_direct, gdir),
        )
    ]
    outs = RowCopies([(ingrad, input_grad)], out_sems, blocks)
    for c in ins:
        c.wait()

    def one(i, carried):
        rows = big_rows(i)
        ingrad[rows, :] = gsum[rows, :] + mul_nt(gproj[rows, :], win[...])

        @pl.when(side == 0)
        def _():
            ingrad[rows, :] += gdir[rows, :]

        @pl.when(side == 1)
        def _():
            running = column(halting[:, rows].astype(F32))
            ingrad[rows, :] += (1.0 - running) * cot[rows, :]

        outs.start(i)
        return carried

    lax.fori_loop(0, blocks, one, 0)
    outs.wait()


def run_self_close(side, halting, cotangent, grad_direct, grad_sum, grad_projected, weight_in):
    n, d = cotangent.shape
    V = pltpu.VMEM
    sem = pltpu.SemaphoreType.DMA
    return call(
        self_close_kernel,
        [SMEM, VMEM, ANY, ANY, HELD, HELD, ANY],
        [(shape((n, d), F32), ANY)],
        [
            V((n, d), F32), V((n, d), F32), V((d, 3 * d), BF16), V((n, d), F32),
            sem((3,)), sem((1, n // BIG)),
        ],
        2_000_000_000, 12_000_000, name="self_close",
    )(side, halting, cotangent, grad_direct, grad_sum, grad_projected, weight_in)[0]


def mul_tn(left, right):
    return lax.dot_general(left, right, (((0,), (0,)), ((), ())), preferred_element_type=F32)


def half_of(value, index, axis=0):
    size = value.shape[axis] // 2
    return lax.dynamic_slice_in_dim(value, index * size, size, axis)


def exchange(value, bit):
    return lax.ppermute(value, "dp", [(i, i ^ bit) for i in range(lax.axis_size("dp"))])


def own_of(bit):
    return (lax.axis_index("dp") // bit) % 2


def joined(value, came, bit):
    own = own_of(bit)
    return jnp.concatenate([jnp.where(own == 0, value, came), jnp.where(own == 0, came, value)], axis=0)


class Flow:
    def __init__(self, values, swapped):
        bits = [1 << b for b in range(1, lax.axis_size("dp").bit_length() - 1)]
        if swapped and len(bits) > 1:
            bits[0], bits[1] = bits[1], bits[0]
        self.steps = [(b, True) for b in bits] + [(b, False) for b in reversed(bits)] + [(1, False)]
        self.sizes = [v.shape[0] // 2 for v in values]
        own = own_of(1)
        self.kept = jnp.concatenate([half_of(v, own) for v in values], axis=0)
        self.sent = jnp.concatenate([half_of(v, 1 - own) for v in values], axis=0)

    def fold(self):
        came = exchange(self.sent, 1)
        self.value = (self.kept.astype(F32) + came.astype(F32)).astype(BF16)

    @property
    def left(self):
        return len(self.steps)

    def operand(self):
        bit, halves = self.steps[0]
        return half_of(self.value, 1 - own_of(bit)) if halves else self.value

    def land(self, came):
        bit, halves = self.steps.pop(0)
        if halves:
            kept = half_of(self.value, own_of(bit))
            self.value = (kept.astype(F32) + came.astype(F32)).astype(BF16)
        elif self.left:
            self.value = joined(self.value, came, bit)
        else:
            self.came = came

    def pieces(self):
        out, at = [], 0
        for size in self.sizes:
            out.append(joined(self.value[at : at + size], self.came[at : at + size], 1).astype(F32))
            at += size
        return out


def stage(flows, work=None, *inputs, beside=None):
    flows = [f for f in flows if f.left]
    sent, values, inputs = lax.optimization_barrier(
        ([f.operand() for f in flows], [f.value for f in flows], inputs)
    )
    came = [exchange(s, f.steps[0][0]) for s, f in zip(sent, flows)]
    out = None
    if work is not None:
        out = work(*inputs)
        came, values, out, beside = lax.optimization_barrier((came, values, out, beside))
    for flow, value, piece in zip(flows, values, came):
        flow.value = value
        flow.land(piece)
    return out if beside is None else (out, beside)


def body(
    tokens, cotangent, lengths, halting, attention_in, attention_out, cross_first, cross_second,
    expand_weight, expand_bias, contract_weight, contract_bias, norm_gain, norm_bias,
):
    side_index = lax.axis_index("half")
    side = side_index.astype(jnp.int32).reshape((1,))
    tok, cot = tokens[0, 0], cotangent[0, 0]
    lens = lengths[:, 0]
    halt = halting[0]
    w_in, w_out, w_one, w_two = attention_in[0], attention_out[0], cross_first[0], cross_second[0]
    w1, w2 = expand_weight[0], contract_weight[0]
    gains, shifts = norm_gain[0], norm_bias[0]
    n, d = tok.shape
    ff = w1.shape[1]
    there, back = [(0, 1)], [(1, 0)]
    source_pair = lax.ppermute(jnp.concatenate([w_one, w_two], axis=0), "half", there)
    (
        start_low, projected, attended, logs_a, first_sum, memory, memory_low_a, keys,
        held_w1, held_w2, held_out, held_start, held_proj, held_keys, held_turned,
    ) = run_first(side, lens, tok, halt, w_in, w_out, w1, expand_bias, w2, contract_bias, gains, shifts)
    memory_a = lax.ppermute(memory_low_a, "half", there)
    attended, logs_b, first_sum, memory, memory_low_b = run_second(
        side, lens, tok, halt, held_out, held_w1, expand_bias, held_w2, contract_bias, gains, shifts,
        held_proj, held_keys, held_turned, held_start, attended, first_sum, memory,
    )
    memory_a, memory_low_b = lax.optimization_barrier((memory_a, memory_low_b))
    memory_b = lax.ppermute(memory_low_b, "half", there)
    (
        result, hidden, branch, grad_before, ffn_in, grad_first, grad_memory_a, grad_memory_b,
        pairs_low, crossed, grad_cross, first_low, grad_query, kept, small,
    ) = run_middle(
        side, lens, tok, halt, cot, first_sum, memory_a, memory_b, source_pair[:d], source_pair[d:], w_one, w_two,
        w1, expand_bias, w2, contract_bias, gains, shifts, memory,
    )
    grad_a = lax.ppermute(grad_memory_a, "half", back)
    grad_a, grad_memory_b = lax.optimization_barrier((grad_a, grad_memory_b))
    grad_b = lax.ppermute(grad_memory_b, "half", back)
    wide = (w1, w2, w_out, gains, shifts)
    *earlier, inner_a, our_one, our_two, for_source = run_back(
        0, side, halt, cot, first_sum, grad_a, kept, attended, *wide, branch, grad_before, grad_first, small,
        (first_low, crossed, memory_a, memory_b, grad_query, grad_cross, pairs_low),
    )
    ours = (our_one, our_two)
    branch, grad_before, small, *earlier = earlier
    grad_b, small, for_source = lax.optimization_barrier((grad_b, small, for_source))
    from_target = lax.ppermute(for_source, "half", back)
    branch, grad_before, small, grad_direct, gsum, gmix, gatt, inner_b = run_back(
        1, side, halt, cot, first_sum, grad_b, kept, attended, *wide, branch, grad_before, grad_first, small,
        (*earlier, inner_a),
    )
    contract = Flow([mul_tn(hidden, branch).astype(BF16)], False)
    contract.fold()
    expand = Flow([mul_tn(ffn_in, grad_before).astype(BF16)], True)
    expand.fold()

    def heads(g, inner_one, inner_two):
        return run_self_heads(
            0, d // 128, side, lens, projected, g, (logs_a, logs_b), (inner_one, inner_two), keys
        )

    grad_projected, from_target = stage(
        [contract, expand], heads, gatt, inner_a, inner_b, beside=from_target
    )
    later = []

    def products(gproj, mix, theirs, small_sums):
        weights_in = Flow([mul_tn(start_low, gproj).astype(BF16)], True)
        weights_in.fold()
        low_small = jnp.concatenate(
            [small_sums.astype(BF16), jnp.zeros((16 * lax.axis_size("dp") - SMALL_ROWS, d), BF16)], axis=0
        )
        rest = Flow(
            [
                mul_tn(attended, mix).astype(BF16),
                jnp.where(side_index == 0, theirs[:d], ours[0]),
                jnp.where(side_index == 0, theirs[d:], ours[1]),
                low_small,
            ],
            False,
        )
        rest.fold()
        later.extend([weights_in, rest])
        return weights_in.value, rest.value

    values = stage([contract, expand], products, grad_projected, gmix, from_target, small)
    weights_in, rest = later
    weights_in.value, rest.value = values

    def close(gproj):
        return run_self_close(side, halt, cot, grad_direct, gsum, gproj, w_in)

    flows = [contract, expand, weights_in, rest]
    input_grad = stage(flows, close, grad_projected)
    while contract.left:
        stage(flows)
    ended = [contract.value, contract.came, expand.value, expand.came]

    def widen(*arrays):
        contract.value, contract.came, expand.value, expand.came = arrays
        return contract.pieces()[0], expand.pieces()[0]

    contract_out, expand_out = stage(flows, widen, *ended)
    while rest.left:
        stage(flows)
    out_out, first_out, second_out, small_out = rest.pieces()
    small = small_out[:SMALL_ROWS]
    return (
        result[None, None],
        input_grad[None, None],
        weights_in.pieces()[0][None],
        out_out[None],
        first_out[None],
        second_out[None],
        expand_out[None],
        small[8 : 8 + ff // d].reshape(1, ff),
        contract_out[None],
        small[6:7],
        small[0:3][None],
        small[3:6][None],
    )


def solution(mesh):
    placed = (
        P("half", "dp", None, None),
        P("half", "dp", None, None),
        P(None, "dp", None),
        P("half", "dp", None),
        P("half", None, None),
        P("half", None, None),
        P("half", None, None),
        P("half", None, None),
        P("half", None, None),
        P("half", None),
        P("half", None, None),
        P("half", None),
        P("half", None, None),
        P("half", None, None),
    )
    return jax.shard_map(
        body,
        mesh=mesh,
        in_specs=placed,
        out_specs=(
            P("half", "dp", None, None),
            P("half", "dp", None, None),
            P("half", None, None),
            P("half", None, None),
            P("half", None, None),
            P("half", None, None),
            P("half", None, None),
            P("half", None),
            P("half", None, None),
            P("half", None),
            P("half", None, None),
            P("half", None, None),
        ),
        check_vma=False,
    )
```
